512 devices in a mesh: gx: 16 (over y, z_hi), gy: 8 (over x, core), gz: 4 (over z_lo).
Axes of the slice: x: 4, y: 8, z: 8 (z_hi: 2, z_lo: 4; z = z_hi * 4 + z_lo), core: 2. Of those that a mesh axis runs over, the one named last changes fastest.
Arguments:
- volume: bfloat16 [4, 32, 64, 512], P(None, 'gx', 'gy', 'gz'), may hold values from -6 to 6
- w_first: bfloat16 [32, 3, 3, 3, 4], replicated, may hold values from -0.625 to 0.625
- w_second: bfloat16 [32, 3, 3, 3, 32], replicated, may hold values from -0.21875 to 0.21875
- w_coarse: bfloat16 [64, 3, 3, 3, 32], replicated, may hold values from -0.21875 to 0.21875
- skip_cotangent: bfloat16 [32, 32, 64, 512], P(None, 'gx', 'gy', 'gz'), may hold values from -1.796875 to 1.796875
- coarse_cotangent: bfloat16 [64, 16, 32, 256], P('gz', 'gx', 'gy'), may hold values from -6 to 6
Outputs:
- skip: bfloat16 [32, 32, 64, 512], P(None, 'gx', 'gy', 'gz')
- coarse: bfloat16 [64, 16, 32, 256], P('gz', 'gx', 'gy')
- volume_grad: bfloat16 [4, 32, 64, 512], P(None, 'gx', 'gy', 'gz')
- first_wgrad: float32 [32, 3, 3, 3, 4], replicated
- second_wgrad: float32 [32, 3, 3, 3, 32], replicated
- coarse_wgrad: float32 [64, 3, 3, 3, 32], replicated
The draws below stay inside these ranges and needn't reach their ends.
All inputs are finite; a program needn't handle non-finite values.
Results may differ from the reference program's by a relative error of at most 0.014.
Values may be sent and summed in bfloat16 or wider, within the bound.
No kernel may reach another device: no remote copies, remote signals or barrier semaphores. Data moves between devices by JAX's collectives and lax.ppermute only.
A program may use at most 64 MiB of HBM per device.

```python
import math
import jax
import jax.numpy as jnp
from jax import lax

CIN = 4
C1 = 32
C2 = 64
NX = 32
NY = 64
NZ = 512


def steps_of(own_key, extent, shards, low, top_value):
    loudness, own = 1.0, jax.random.fold_in(own_key, 6)
    for dim, parts in shards:
        heights = jnp.exp(jax.random.uniform(jax.random.fold_in(own, dim), (parts,), jnp.float32, low / len(shards), top_value / len(shards)))
        loudness = loudness * jnp.repeat(heights, extent[dim] // parts).reshape([-1 if axis == dim else 1 for axis in range(len(extent))])
    return loudness


def normal_values(rng, shape, scale, bound, pieces=(), held_as=jnp.bfloat16):
    level = steps_of(rng, shape, pieces, -0.22, 0.18) if pieces else 1.0
    entries = jax.random.normal(rng, shape, jnp.float32) * scale * level
    return jnp.minimum(jnp.maximum(entries, -bound), bound).astype(held_as)


def setup_inputs(seed: int = 0) -> dict:
    key_of = jax.random.split(jax.random.key(seed), 7)
    return {
        "volume": normal_values(key_of[0], (CIN, NX, NY, NZ), 1.0, 6.0, ((1, 16), (2, 8), (3, 4))),
        "w_first": normal_values(key_of[1], (C1, 3, 3, 3, CIN), (27 * CIN) ** -0.5, 0.625),
        "w_second": normal_values(key_of[2], (C1, 3, 3, 3, C1), (27 * C1) ** -0.5, 0.21875),
        "w_coarse": normal_values(key_of[3], (C2, 3, 3, 3, C1), (27 * C1) ** -0.5, 0.21875),
        "skip_cotangent": normal_values(key_of[4], (C1, NX, NY, NZ), 0.3, 1.796875, ((1, 16), (2, 8), (3, 4))),
        "coarse_cotangent": normal_values(key_of[5], (C2, NX // 2, NY // 2, NZ // 2), 1.0, 6.0, ((0, 4), (1, 16), (2, 8))),
    }


def convolve(values, weight):
    result = lax.conv_general_dilated(values[None].astype(jnp.float32), weight.astype(jnp.float32), (1, 1, 1), 'SAME', dimension_numbers=('NCDHW', 'ODHWI', 'NCDHW'), precision=lax.Precision.HIGHEST)
    return result[0]

def slope(values):
    sigmoid_value = jax.nn.sigmoid(values)
    return sigmoid_value * (1.0 + values * (1.0 - sigmoid_value))

def backward(values, weight, gradient):
    primal, pullback = jax.vjp(convolve, values.astype(jnp.float32), weight.astype(jnp.float32))
    return pullback(gradient.astype(jnp.float32))

def expand(values):
    chans, extent_a, extent_b, extent_c = values.shape
    wide = jnp.broadcast_to(values[:, :, None, :, None, :, None], (chans, extent_a, 2, extent_b, 2, extent_c, 2))
    return wide.reshape(chans, 2 * extent_a, 2 * extent_b, 2 * extent_c)

def reference(volume, w_first, w_second, w_coarse, skip_cotangent, coarse_cotangent):
    first_pre = convolve(volume, w_first)
    first_act = jax.nn.silu(first_pre).astype(jnp.bfloat16)
    second_pre = convolve(first_act, w_second)
    skip = jax.nn.silu(second_pre).astype(jnp.bfloat16)
    chans, extent_a, extent_b, extent_c = skip.shape
    blocks = skip.astype(jnp.float32).reshape(chans, extent_a // 2, 2, extent_b // 2, 2, extent_c // 2, 2)
    pooled = lax.optimization_barrier(jnp.mean(blocks, axis=(2, 4, 6))).astype(jnp.bfloat16)
    coarse_pre = convolve(pooled, w_coarse)
    coarse = jax.nn.silu(coarse_pre).astype(jnp.bfloat16)
    coarse_grad = (coarse_cotangent.astype(jnp.float32) * slope(coarse_pre)).astype(jnp.bfloat16)
    pooled_grad, coarse_raw = backward(pooled, w_coarse, coarse_grad)
    second_grad = ((skip_cotangent.astype(jnp.float32) + expand(pooled_grad) / 8.0) * slope(second_pre)).astype(jnp.bfloat16)
    first_back, second_raw = backward(first_act, w_second, second_grad)
    first_grad = (first_back * slope(first_pre)).astype(jnp.bfloat16)
    volume_back, first_raw = backward(volume, w_first, first_grad)
    factor = 1.0 / math.sqrt(extent_a * extent_b * extent_c)
    return (skip, coarse, volume_back.astype(jnp.bfloat16), first_raw * factor, second_raw * factor, coarse_raw * factor)
```

```python
import math

import jax
import jax.numpy as jnp
from jax import lax
from jax.sharding import PartitionSpec as P

AXES = ("gx", "gy", "gz")


def shifted(block, axis, step):
    count = lax.axis_size(axis)
    pairs = [(i, i + step) for i in range(count) if 0 <= i + step < count]
    return lax.ppermute(block, axis, pairs)


def halo(cells, axis, dim, width):
    extent = cells.shape[dim]
    before, after = [], []
    for step in range(1, -(-width // extent) + 1):
        part = min(extent, width - (step - 1) * extent)
        tail = lax.slice_in_dim(cells, extent - part, extent, axis=dim)
        head = lax.slice_in_dim(cells, 0, part, axis=dim)
        before.insert(0, shifted(tail, axis, step))
        after.append(shifted(head, axis, -step))
    return jnp.concatenate(before + [cells] + after, axis=dim)


def trim(cells, amounts):
    ends = [extent - amount for extent, amount in zip(cells.shape[1:], amounts)]
    return lax.slice(cells, (0,) + tuple(amounts), (cells.shape[0],) + tuple(ends))


def inside(extents, margins):
    mask = None
    for dim, (axis, extent, margin) in enumerate(zip(AXES, extents, margins)):
        own = extent - 2 * margin
        first = lax.axis_index(axis) * own - margin
        total = lax.axis_size(axis) * own
        place = first + lax.broadcasted_iota(jnp.int32, tuple(extents), dim)
        here = (place >= 0) & (place < total)
        mask = here if mask is None else mask & here
    return mask


def masked(values, margins):
    return jnp.where(inside(values.shape[1:], margins)[None], values, 0.0)


def taps(padded):
    ny, nz = padded.shape[2] - 2, padded.shape[3] - 2
    return jnp.concatenate(
        [padded[:, :, j : j + ny, k : k + nz] for j in range(3) for k in range(3)], axis=0
    )


def convolve(tapped, weight):
    outputs, chans = weight.shape[0], weight.shape[4]
    nx, ny, nz = tapped.shape[1:]
    matrix = jnp.transpose(weight, (1, 0, 2, 3, 4)).reshape(3 * outputs, 9 * chans)
    flat = jnp.dot(
        matrix, tapped.reshape(9 * chans, nx * ny * nz), preferred_element_type=jnp.float32
    )
    parts = flat.reshape(3, outputs, nx, ny, nz)
    return parts[0, :, : nx - 2] + parts[1, :, 1 : nx - 1] + parts[2, :, 2:]


def kernel_grad(gradient, tapped):
    outputs = gradient.shape[0]
    rows = jnp.concatenate(
        [jnp.pad(gradient, ((0, 0), (i, 2 - i), (0, 0), (0, 0))) for i in range(3)], axis=0
    )
    return lax.dot_general(
        rows.reshape(3 * outputs, -1),
        tapped.reshape(tapped.shape[0], -1),
        (((1,), (1,)), ((), ())),
        preferred_element_type=jnp.float32,
    )


def flipped(weight):
    return jnp.transpose(weight[:, ::-1, ::-1, ::-1, :], (4, 1, 2, 3, 0))


def slope(values):
    sigmoid_value = jax.nn.sigmoid(values)
    return sigmoid_value * (1.0 + values * (1.0 - sigmoid_value))


def expand(values):
    chans, extent_a, extent_b, extent_c = values.shape
    wide = jnp.broadcast_to(
        values[:, :, None, :, None, :, None], (chans, extent_a, 2, extent_b, 2, extent_c, 2)
    )
    return wide.reshape(chans, 2 * extent_a, 2 * extent_b, 2 * extent_c)


def to_rows(matrix):
    lanes = -(-matrix.shape[1] // 128) * 128
    wide = jnp.pad(matrix, ((0, 0), (0, lanes - matrix.shape[1])))
    return [wide[:, start : start + 128] for start in range(0, lanes, 128)]


def from_rows(rows, outputs, chans):
    lanes = -(-9 * chans // 128)
    height = 3 * outputs
    pieces = [rows[n * height : (n + 1) * height] for n in range(lanes)]
    matrix = jnp.concatenate(pieces, axis=1)[:, : 9 * chans]
    return jnp.transpose(matrix.reshape(3, outputs, 3, 3, chans), (1, 0, 2, 3, 4))


def swap(blocks, axes):
    return lax.all_to_all(blocks, axes, split_axis=0, concat_axis=0, tiled=True)


def total_over_mesh(matrices):
    plane = ("gy", "gz")
    count = lax.axis_size("gy") * lax.axis_size("gz")
    line = lax.axis_size("gx")
    rows = jnp.concatenate([piece for matrix in matrices for piece in to_rows(matrix)], axis=0)
    share = -(-rows.shape[0] // (8 * count)) * 8
    rows = jnp.pad(rows, ((0, share * count - rows.shape[0]), (0, 0)))
    part = jnp.sum(swap(rows.reshape(count, share, 128), plane), axis=0)
    part = jnp.sum(swap(jnp.broadcast_to(part, (line, share, 128)), "gx"), axis=0)
    whole = swap(jnp.broadcast_to(part, (count, share, 128)), plane)
    return whole.reshape(count * share, 128)


def local(volume, w_first, w_second, w_coarse, skip_cotangent, coarse_cotangent):
    wide_volume = halo(halo(halo(volume, "gx", 1, 4), "gy", 2, 4), "gz", 3, 8)
    sides = lax.axis_size("gz")
    depth = coarse_cotangent.shape[3] // sides
    guarded = jnp.pad(coarse_cotangent, ((0, 0), (0, 0), (0, 0), (2, 2)))
    sent = jnp.concatenate(
        [guarded[..., n * depth : n * depth + depth + 4] for n in range(sides)], axis=0
    )
    returned = swap(sent, "gz")
    wide_cotangent = halo(halo(halo(skip_cotangent, "gx", 1, 2), "gy", 2, 2), "gz", 3, 2)

    volume_taps = taps(wide_volume)
    first_pre = convolve(volume_taps, w_first)
    first_act = masked(jax.nn.silu(first_pre), (3, 3, 7)).astype(jnp.bfloat16)
    second_pre = convolve(taps(first_act), w_second)
    wide_skip = jax.nn.silu(second_pre).astype(jnp.bfloat16)
    skip = trim(wide_skip, (2, 2, 6))
    chans, extent_a, extent_b, extent_c = wide_skip.shape
    blocks = wide_skip.astype(jnp.float32).reshape(
        chans, extent_a // 2, 2, extent_b // 2, 2, extent_c // 2, 2
    )
    pooled = masked(jnp.mean(blocks, axis=(2, 4, 6)), (1, 1, 3)).astype(jnp.bfloat16)
    pooled_taps = taps(pooled)
    coarse_pre = convolve(pooled_taps, w_coarse)
    coarse_local = jax.nn.silu(coarse_pre[..., 2:-2]).astype(jnp.bfloat16)
    coarse = lax.all_to_all(coarse_local, "gz", split_axis=0, concat_axis=3, tiled=True)
    coarse_grad = (returned.astype(jnp.float32) * slope(coarse_pre)).astype(jnp.bfloat16)
    coarse_raw = kernel_grad(coarse_grad[..., 2:-2], pooled_taps[..., 2:-2])

    wide_grad = halo(halo(coarse_grad, "gx", 1, 2), "gy", 2, 2)
    pooled_grad = convolve(taps(wide_grad), flipped(w_coarse))
    second_grad = masked(
        (wide_cotangent.astype(jnp.float32) + expand(pooled_grad) / 8.0)
        * slope(second_pre[..., 4:-4]),
        (2, 2, 2),
    ).astype(jnp.bfloat16)
    second_raw = kernel_grad(trim(second_grad, (2, 2, 2)), taps(trim(first_act, (2, 2, 6))))
    first_back = convolve(taps(second_grad), flipped(w_second))
    first_grad = masked(
        first_back * slope(trim(first_pre, (2, 2, 6))), (1, 1, 1)
    ).astype(jnp.bfloat16)
    first_raw = kernel_grad(trim(first_grad, (1, 1, 1)), taps(trim(wide_volume, (3, 3, 7))))
    volume_grad = convolve(taps(first_grad), flipped(w_first)).astype(jnp.bfloat16)

    rows = total_over_mesh((first_raw, second_raw, coarse_raw))
    voxels = skip.shape[1] * skip.shape[2] * skip.shape[3]
    for axis in AXES:
        voxels = voxels * lax.axis_size(axis)
    factor = 1.0 / math.sqrt(voxels)
    grads, start = [], 0
    for weight in (w_first, w_second, w_coarse):
        outputs, width = weight.shape[0], weight.shape[4]
        height = 3 * outputs * -(-9 * width // 128)
        grads.append(from_rows(rows[start : start + height], outputs, width) * factor)
        start += height
    return (skip, coarse, volume_grad, *grads)


def solution(mesh):
    in_specs = (
        P(None, "gx", "gy", "gz"),
        P(),
        P(),
        P(),
        P(None, "gx", "gy", "gz"),
        P("gz", "gx", "gy", None),
    )
    out_specs = (
        P(None, "gx", "gy", "gz"),
        P("gz", "gx", "gy", None),
        P(None, "gx", "gy", "gz"),
        P(),
        P(),
        P(),
    )
    return jax.shard_map(local, mesh=mesh, in_specs=in_specs, out_specs=out_specs, check_vma=False)
```

```python
import math

import jax
import jax.numpy as jnp
from jax import lax
from jax.experimental import pallas as pl
from jax.experimental.pallas import tpu as pltpu
from jax.sharding import PartitionSpec as P

AXES = ("gx", "gy", "gz")
LANES = 256
BF = jnp.bfloat16
F32 = jnp.float32


def shifted(block, axis, step):
    count = lax.axis_size(axis)
    pairs = [(i, i + step) for i in range(count) if 0 <= i + step < count]
    return lax.ppermute(block, axis, pairs)


def halo(cells, axis, dim, width):
    extent = cells.shape[dim]
    before, after = [], []
    for step in range(1, -(-width // extent) + 1):
        part = min(extent, width - (step - 1) * extent)
        tail = lax.slice_in_dim(cells, extent - part, extent, axis=dim)
        head = lax.slice_in_dim(cells, 0, part, axis=dim)
        before.insert(0, shifted(tail, axis, step))
        after.append(shifted(head, axis, -step))
    return jnp.concatenate(before + [cells] + after, axis=dim)


def slope(values):
    sigmoid_value = jax.nn.sigmoid(values)
    return sigmoid_value * (1.0 + values * (1.0 - sigmoid_value))


def silu(values):
    return values * jax.nn.sigmoid(values)


def store_taps(ref, place, values):
    chans, lanes = values.shape
    ref[place + (slice(0, chans),)] = pltpu.roll(values, 1, 1).astype(BF)
    ref[place + (slice(chans, 2 * chans),)] = values.astype(BF)
    ref[place + (slice(2 * chans, 3 * chans),)] = pltpu.roll(values, lanes - 1, 1).astype(BF)


def rows_at(ref, plane, row):
    part = ref[plane, row - 1 : row + 2]
    return part.reshape(part.shape[0] * part.shape[1], part.shape[2])


def dot(left, right):
    return jnp.dot(left, right, preferred_element_type=F32)


def dot_lanes(left, right):
    return lax.dot_general(left, right, (((1,), (1,)), ((), ())), preferred_element_type=F32)


def lane_mask(lanes, first, low, high):
    place = first + lax.broadcasted_iota(jnp.int32, (1, lanes), 1)
    return jnp.where((place >= low) & (place < high), 1.0, 0.0).astype(F32)


def keep(values, lanes_ok, *bounds):
    good = None
    for place, limit in bounds:
        here = (place >= 0) & (place < limit)
        good = here if good is None else good & here
    mask = lanes_ok * jnp.where(good, 1.0, 0.0).astype(F32)
    return jnp.where(mask > 0.5, values, 0.0)


def spread_conv(acc, weights, tapped, planes, rows, outputs, shift):
    matrix = weights[...]

    def one(n, carry):
        plane = planes[0] + n
        for row in range(*rows):
            summed = dot(matrix, rows_at(tapped, plane, row))
            for i in range(3):
                place = plane + shift - i
                acc[place, row] = acc[place, row] + summed[i * outputs : (i + 1) * outputs]
        return carry

    lax.fori_loop(0, planes[1] - planes[0], one, 0)


def clear(acc):
    def one(n, carry):
        acc[n] = jnp.zeros(acc.shape[1:], acc.dtype)
        return carry

    lax.fori_loop(0, acc.shape[0], one, 0)


def forward_kernel(
    sizes, offs, vol, w1, w2, w3, cot, pool,
    skip_o, coarse_o, cgrad_o, craw_o, fpre_o, spre_o, t1_o, t2_o,
    t1, acc1, t2, acc2, fine, t3,
):
    nx, ny, nz = sizes
    ox, oy, oz = offs[0], offs[1], offs[2]
    fine_ok = lane_mask(LANES, oz - 8, 0, nz)
    coarse_ok = lane_mask(128, oz // 2 - 4, 0, nz // 2)

    def volume_taps(x, carry):
        for y in range(16):
            store_taps(t1, (x, y), vol[x, y].astype(F32))
        return carry

    lax.fori_loop(0, 10, volume_taps, 0)
    clear(acc1)
    spread_conv(acc1, w1, t1, (0, 10), (1, 15), 32, 2)

    def first(n, carry):
        x = n + 1
        for y in range(1, 15):
            act = silu(acc1[x + 1, y])
            act = keep(act, fine_ok, (ox + x - 4, nx), (oy + y - 4, ny))
            store_taps(t2, (x, y), act.astype(BF).astype(F32))
        return carry

    lax.fori_loop(0, 8, first, 0)
    clear(acc2)
    spread_conv(acc2, w2, t2, (1, 9), (2, 14), 32, 2)

    def second(n, carry):
        for y in range(12):
            pre = acc2[n + 3, y + 2]
            spre_o[n, y] = pre
            fine[n, y] = silu(pre).astype(BF)
        return carry

    lax.fori_loop(0, 6, second, 0)

    def passed(n, carry):
        for y in range(10):
            fpre_o[n, y] = acc1[n + 4, y + 3]
            t1_o[n, y] = t1[n + 3, y + 3]
            t2_o[n, y] = t2[n + 3, y + 3]
        return carry

    lax.fori_loop(0, 4, passed, 0)
    for x in range(2):
        for y in range(8):
            whole = pltpu.roll(fine[x + 2, y + 2].astype(F32), LANES - 8, 1)
            skip_o[x, y] = whole[:, :128].astype(BF)

    matrix = pool[...]
    for x in range(3):
        for y in range(6):
            cube = fine[2 * x : 2 * x + 2, 2 * y : 2 * y + 2].reshape(128, LANES)
            parts = dot(cube, matrix)
            mean = (parts[0:32] + parts[32:64] + parts[64:96] + parts[96:128]) * 0.125
            mean = keep(mean, coarse_ok, (ox // 2 + x - 1, nx // 2), (oy // 2 + y - 1, ny // 2))
            store_taps(t3, (x, y), mean.astype(BF).astype(F32))

    own = lane_mask(128, 0, 4, 68)
    raw = [jnp.zeros((64, 288), F32) for _ in range(3)]
    for y in range(4):
        pre = jnp.zeros((64, 128), F32)
        for i in range(3):
            pre = pre + dot(w3[i], rows_at(t3, i, y + 1))
        coarse_o[y] = silu(pre).astype(BF)
        grad = cot[y].astype(F32) * slope(pre)
        cgrad_o[y] = grad.astype(BF)
        mine = jnp.where(own > 0.5, grad, 0.0).astype(BF)
        for i in range(3):
            raw[i] = raw[i] + dot_lanes(mine, rows_at(t3, i, y + 1))
    for i in range(3):
        craw_o[i * 64 : (i + 1) * 64] = raw[i]


def backward_kernel(
    sizes, offs, cgrad, spre, fpre, cot, t1, t2, w3, w2, w1, spread,
    vgrad_o, sraw_o, fraw_o,
    t4, acc4, t5, own5, acc5, t6, own6,
):
    nx, ny, nz = sizes
    ox, oy, oz = offs[0], offs[1], offs[2]
    fine_ok = lane_mask(LANES, oz - 8, 0, nz)
    own_ok = lane_mask(LANES, 0, 8, 136)

    for x in range(5):
        for y in range(8):
            store_taps(t4, (x, y), cgrad[x, y].astype(F32))
    clear(acc4)
    spread_conv(acc4, w3, t4, (0, 5), (1, 7), 32, 2)

    own5[0] = jnp.zeros(own5.shape[1:], BF)
    own5[1] = jnp.zeros(own5.shape[1:], BF)
    own5[4] = jnp.zeros(own5.shape[1:], BF)
    own5[5] = jnp.zeros(own5.shape[1:], BF)
    own6[0] = jnp.zeros(own6.shape[1:], BF)
    own6[1] = jnp.zeros(own6.shape[1:], BF)
    own6[4] = jnp.zeros(own6.shape[1:], BF)
    own6[5] = jnp.zeros(own6.shape[1:], BF)
    matrix = spread[...]

    def second(n, carry):
        for cy in range(6):
            value = acc4[n + 2, cy + 1]
            high = value.astype(BF)
            low = (value - high.astype(F32)).astype(BF)
            wide = dot(high, matrix) + dot(low, matrix)
            for dx in range(2):
                for dy in range(2):
                    x, y = 2 * n + dx, 2 * cy + dy
                    grad = (cot[x, y].astype(F32) + wide) * slope(spre[x, y])
                    grad = keep(grad, fine_ok, (ox + x - 2, nx), (oy + y - 2, ny))
                    store_taps(t5, (x, y), grad.astype(BF).astype(F32))
        return carry

    lax.fori_loop(0, 3, second, 0)
    for x in range(2):
        for y in range(8):
            mine = t5[x + 2, y + 2, 32:64].astype(F32)
            own5[x + 2, y] = jnp.where(own_ok > 0.5, mine, 0.0).astype(BF)

    clear(acc5)
    spread_conv(acc5, w2, t5, (0, 6), (1, 11), 32, 2)

    def first(n, carry):
        for y in range(10):
            grad = acc5[n + 2, y + 1] * slope(fpre[n, y])
            grad = keep(grad, fine_ok, (ox + n - 1, nx), (oy + y - 1, ny))
            store_taps(t6, (n, y), grad.astype(BF).astype(F32))
        return carry

    lax.fori_loop(0, 4, first, 0)
    for x in range(2):
        for y in range(8):
            mine = t6[x + 1, y + 1, 32:64].astype(F32)
            own6[x + 2, y] = jnp.where(own_ok > 0.5, mine, 0.0).astype(BF)

    sraw_o[...] = jnp.zeros(sraw_o.shape, F32)
    fraw_o[...] = jnp.zeros(fraw_o.shape, F32)

    def weight_grads(n, carry):
        second_sum = jnp.zeros(sraw_o.shape, F32)
        first_sum = jnp.zeros(fraw_o.shape, F32)
        for y in range(8):
            left = jnp.concatenate([own5[n + 2, y], own5[n + 1, y], own5[n, y]], axis=0)
            second_sum = second_sum + dot_lanes(left, rows_at(t2, n, y + 1))
            left = jnp.concatenate([own6[n + 2, y], own6[n + 1, y], own6[n, y]], axis=0)
            first_sum = first_sum + dot_lanes(left, rows_at(t1, n, y + 1))
        sraw_o[...] += second_sum
        fraw_o[...] += first_sum
        return carry

    lax.fori_loop(0, 4, weight_grads, 0)

    for x in range(2):
        for y in range(8):
            total = jnp.zeros((16, LANES), F32)
            for i in range(3):
                total = total + dot(w1[i], rows_at(t6, x + i, y + 1))
            vgrad_o[x, y] = pltpu.roll(total, LANES - 8, 1)[:, :128].astype(BF)


def flipped(weight):
    return jnp.transpose(weight[:, ::-1, ::-1, ::-1, :], (4, 1, 2, 3, 0))


def stacked(weight):
    outputs, chans = weight.shape[0], weight.shape[4]
    return jnp.transpose(weight, (1, 0, 2, 3, 4)).reshape(3, outputs, 9 * chans)


def swap(blocks, axes):
    return lax.all_to_all(blocks, axes, split_axis=0, concat_axis=0, tiled=True)


def added(blocks):
    return lax.optimization_barrier(jnp.sum(blocks.astype(F32), axis=0)).astype(BF)


def total_over_mesh(rows):
    plane = ("gy", "gz")
    count = lax.axis_size("gy") * lax.axis_size("gz")
    line = lax.axis_size("gx")
    share = -(-rows.shape[0] // (8 * count)) * 8
    rows = jnp.pad(rows.astype(BF), ((0, share * count - rows.shape[0]), (0, 0)))
    part = added(swap(rows.reshape(count, share, 128), plane))
    part = added(swap(jnp.broadcast_to(part, (line, share, 128)), "gx"))
    whole = swap(jnp.broadcast_to(part, (count, share, 128)), plane)
    return whole.reshape(count * share, 128).astype(F32)


def grads_over_mesh(first_raw, second_raw, coarse_raw):
    wide = jnp.concatenate([coarse_raw, second_raw], axis=0)
    height = wide.shape[0]
    piece = height // 4
    rest = jnp.concatenate(
        [wide[n * piece : (n + 1) * piece, 256:288] for n in range(4)], axis=1
    )
    thin = first_raw.reshape(96, 9, 16)[:, :, :4].reshape(96, 36)
    rows = jnp.concatenate(
        [wide[:, :128], wide[:, 128:256], rest, jnp.pad(thin, ((0, 0), (0, 92)))], axis=0
    )
    rows = total_over_mesh(rows)
    rest = rows[2 * height : 2 * height + piece]
    rest = jnp.concatenate([rest[:, 32 * n : 32 * n + 32] for n in range(4)], axis=0)
    wide = jnp.concatenate([rows[:height], rows[height : 2 * height], rest], axis=1)
    thin = rows[2 * height + piece : 2 * height + piece + 96, :36]
    return thin, wide[192:], wide[:192]


def weight_form(matrix, outputs, chans):
    return jnp.transpose(matrix.reshape(3, outputs, 3, 3, chans), (1, 0, 2, 3, 4))


def shape(dims, dtype):
    return jax.ShapeDtypeStruct(dims, dtype)


def local(volume, w_first, w_second, w_coarse, skip_cotangent, coarse_cotangent):
    counts = [lax.axis_size(axis) for axis in AXES]
    extents = volume.shape[1:]
    sizes = tuple(count * extent for count, extent in zip(counts, extents))
    offs = jnp.stack([lax.axis_index(axis) * extent for axis, extent in zip(AXES, extents)])
    offs = offs.astype(jnp.int32)

    wide_volume = halo(halo(halo(volume, "gx", 1, 4), "gy", 2, 4), "gz", 3, 8)
    wide_volume = jnp.pad(
        jnp.transpose(wide_volume, (1, 2, 0, 3)), ((0, 0), (0, 0), (0, 12), (0, LANES - 144))
    )
    sides = counts[2]
    depth = coarse_cotangent.shape[3] // sides
    guarded = jnp.pad(coarse_cotangent[:, 0], ((0, 0), (0, 0), (2, 2)))
    sent = jnp.stack([guarded[..., n * depth : n * depth + depth + 4] for n in range(sides)])
    returned = swap(sent, "gz")
    returned = jnp.transpose(returned, (2, 0, 1, 3)).reshape(4, 64, depth + 4)
    returned = jnp.pad(returned, ((0, 0), (0, 0), (2, 128 - 70)))
    rows_cotangent = jnp.transpose(skip_cotangent, (1, 2, 0, 3))
    wide_cotangent = halo(halo(halo(rows_cotangent, "gx", 0, 2), "gy", 1, 2), "gz", 3, 2)
    wide_cotangent = jnp.pad(wide_cotangent, ((0, 0), (0, 0), (0, 0), (6, LANES - 138)))

    fine_place = lax.broadcasted_iota(jnp.int32, (LANES, 128), 0)
    coarse_place = lax.broadcasted_iota(jnp.int32, (LANES, 128), 1)
    pool = jnp.where(fine_place // 2 == coarse_place, 1.0, 0.0).astype(BF)
    spread = jnp.transpose(pool) * 0.125

    thin_first = jnp.pad(w_first, ((0, 0), (0, 0), (0, 0), (0, 0), (0, 12)))
    smem = pl.BlockSpec(memory_space=pltpu.SMEM)
    vmem = pl.BlockSpec(memory_space=pltpu.VMEM)
    skip, coarse_local, coarse_grad, coarse_raw, first_pre, second_pre, taps1, taps2 = (
        pl.pallas_call(
            lambda *refs: forward_kernel(sizes, *refs),
            out_shape=(
                shape((2, 8, 32, 128), BF),
                shape((4, 64, 128), BF),
                shape((4, 64, 128), BF),
                shape((192, 288), F32),
                shape((4, 10, 32, LANES), F32),
                shape((6, 12, 32, LANES), F32),
                shape((4, 10, 48, LANES), BF),
                shape((4, 10, 96, LANES), BF),
            ),
            in_specs=[smem] + [vmem] * 6,
            out_specs=(vmem,) * 8,
            scratch_shapes=[
                pltpu.VMEM((10, 16, 48, LANES), BF),
                pltpu.VMEM((12, 16, 32, LANES), F32),
                pltpu.VMEM((10, 16, 96, LANES), BF),
                pltpu.VMEM((12, 16, 32, LANES), F32),
                pltpu.VMEM((6, 12, 32, LANES), BF),
                pltpu.VMEM((3, 6, 96, 128), BF),
            ],
            compiler_params=pltpu.CompilerParams(vmem_limit_bytes=52 * 2**20),
            cost_estimate=pl.CostEstimate(
                flops=4 * 10**9, bytes_accessed=12 * 10**6, transcendentals=10**6
            ),
            name="forward",
        )(
            offs,
            wide_volume,
            stacked(thin_first).reshape(96, 144),
            stacked(w_second).reshape(96, 288),
            stacked(w_coarse),
            returned,
            pool,
        )
    )
    coarse = coarse_local[:, :, 4 : 4 + depth].reshape(4, sides, 64 // sides, depth)
    coarse = swap(jnp.transpose(coarse, (1, 2, 0, 3)), "gz")
    coarse = jnp.transpose(coarse, (1, 2, 0, 3)).reshape(64 // sides, 1, 4, sides * depth)

    wide_grad = halo(halo(coarse_grad[None], "gx", 0, 2), "gy", 1, 2)
    back_first = jnp.pad(flipped(w_first), ((0, 12),) + ((0, 0),) * 4)
    volume_grad, second_raw, first_raw = pl.pallas_call(
        lambda *refs: backward_kernel(sizes, *refs),
        out_shape=(
            shape((2, 8, 16, 128), BF),
            shape((96, 288), F32),
            shape((96, 144), F32),
        ),
        in_specs=[smem] + [vmem] * 10,
        out_specs=(vmem,) * 3,
        scratch_shapes=[
            pltpu.VMEM((5, 8, 192, 128), BF),
            pltpu.VMEM((7, 8, 32, 128), F32),
            pltpu.VMEM((6, 12, 96, LANES), BF),
            pltpu.VMEM((6, 8, 32, LANES), BF),
            pltpu.VMEM((8, 12, 32, LANES), F32),
            pltpu.VMEM((4, 10, 96, LANES), BF),
            pltpu.VMEM((6, 8, 32, LANES), BF),
        ],
        compiler_params=pltpu.CompilerParams(vmem_limit_bytes=52 * 2**20),
        cost_estimate=pl.CostEstimate(
            flops=2 * 10**9, bytes_accessed=10 * 10**6, transcendentals=10**6
        ),
        name="backward",
    )(
        offs,
        wide_grad,
        second_pre,
        first_pre,
        wide_cotangent,
        taps1,
        taps2,
        stacked(flipped(w_coarse)).reshape(96, 576),
        stacked(flipped(w_second)).reshape(96, 288),
        stacked(back_first),
        spread,
    )

    skip = jnp.transpose(skip, (2, 0, 1, 3))
    volume_grad = jnp.transpose(volume_grad[:, :, :4], (2, 0, 1, 3))
    factor = 1.0 / math.sqrt(sizes[0] * sizes[1] * sizes[2])
    thin, second, wide = grads_over_mesh(first_raw, second_raw, coarse_raw)
    return (
        skip,
        coarse,
        volume_grad,
        weight_form(thin * factor, 32, 4),
        weight_form(second * factor, 32, 32),
        weight_form(wide * factor, 64, 32),
    )


def solution(mesh):
    in_specs = (
        P(None, "gx", "gy", "gz"),
        P(),
        P(),
        P(),
        P(None, "gx", "gy", "gz"),
        P("gz", "gx", "gy", None),
    )
    out_specs = (
        P(None, "gx", "gy", "gz"),
        P("gz", "gx", "gy", None),
        P(None, "gx", "gy", "gz"),
        P(),
        P(),
        P(),
    )
    return jax.shard_map(local, mesh=mesh, in_specs=in_specs, out_specs=out_specs, check_vma=False)
```

```python
import math

import jax
import jax.numpy as jnp
from jax import lax
from jax.experimental import pallas as pl
from jax.experimental.pallas import tpu as pltpu
from jax.sharding import PartitionSpec as P

AXES = ("gx", "gy", "gz")
LANES = 256
BF = jnp.bfloat16
F32 = jnp.float32


def shifted(block, axis, step):
    count = lax.axis_size(axis)
    pairs = [(i, i + step) for i in range(count) if 0 <= i + step < count]
    return lax.ppermute(block, axis, pairs)


def halo(cells, axis, dim, width):
    extent = cells.shape[dim]
    before, after = [], []
    for step in range(1, -(-width // extent) + 1):
        part = min(extent, width - (step - 1) * extent)
        tail = lax.slice_in_dim(cells, extent - part, extent, axis=dim)
        head = lax.slice_in_dim(cells, 0, part, axis=dim)
        before.insert(0, shifted(tail, axis, step))
        after.append(shifted(head, axis, -step))
    return jnp.concatenate(before + [cells] + after, axis=dim)


def slope(values):
    sigmoid_value = jax.nn.sigmoid(values)
    return sigmoid_value * (1.0 + values * (1.0 - sigmoid_value))


def silu(values):
    return values * jax.nn.sigmoid(values)


def store_taps(ref, place, values):
    chans, lanes = values.shape
    ref[place + (slice(0, chans),)] = pltpu.roll(values, 1, 1).astype(BF)
    ref[place + (slice(chans, 2 * chans),)] = values.astype(BF)
    ref[place + (slice(2 * chans, 3 * chans),)] = pltpu.roll(values, lanes - 1, 1).astype(BF)


def rows_at(ref, plane, row):
    part = ref[plane, row - 1 : row + 2]
    return part.reshape(part.shape[0] * part.shape[1], part.shape[2])


def dot(left, right):
    return jnp.dot(left, right, preferred_element_type=F32)


def dot_lanes(left, right):
    return lax.dot_general(left, right, (((1,), (1,)), ((), ())), preferred_element_type=F32)


def lane_mask(lanes, first, low, high):
    place = first + lax.broadcasted_iota(jnp.int32, (1, lanes), 1)
    return jnp.where((place >= low) & (place < high), 1.0, 0.0).astype(F32)


def keep(values, lanes_ok, *bounds):
    good = None
    for place, limit in bounds:
        here = (place >= 0) & (place < limit)
        good = here if good is None else good & here
    mask = lanes_ok * jnp.where(good, 1.0, 0.0).astype(F32)
    return jnp.where(mask > 0.5, values, 0.0)


def spread_conv(acc, weights, tapped, planes, rows, outputs, shift):
    matrix = weights[...]

    def one(n, carry):
        plane = planes[0] + n
        for row in range(*rows):
            summed = dot(matrix, rows_at(tapped, plane, row))
            acc[plane + shift, row] = summed[:outputs]
            for i in (1, 2):
                place = plane + shift - i
                acc[place, row] = acc[place, row] + summed[i * outputs : (i + 1) * outputs]
        return carry

    lax.fori_loop(0, planes[1] - planes[0], one, 0)


def forward_kernel(
    sizes, offs, vol, w1, w2, w3, cot, pool, unread,
    skip_o, coarse_o, cgrad_o, craw_o, fpre_o, spre_o, t1_o, t2_o,
    t1, acc1, t2, acc2, fine, t3,
):
    nx, ny, nz = sizes
    ox, oy, oz = offs[0], offs[1], offs[2]
    fine_ok = lane_mask(LANES, oz - 8, 0, nz)
    coarse_ok = lane_mask(128, oz // 2 - 4, 0, nz // 2)

    def volume_taps(x, carry):
        for y in range(16):
            store_taps(t1, (x, y), vol[x, y].astype(F32))
        return carry

    lax.fori_loop(0, 10, volume_taps, 0)
    spread_conv(acc1, w1, t1, (0, 10), (1, 15), 32, 2)

    def first(n, carry):
        x = n + 1
        for y in range(1, 15):
            act = silu(acc1[x + 1, y])
            act = keep(act, fine_ok, (ox + x - 4, nx), (oy + y - 4, ny))
            store_taps(t2, (x, y), act.astype(BF).astype(F32))
        return carry

    lax.fori_loop(0, 8, first, 0)
    spread_conv(acc2, w2, t2, (1, 9), (2, 14), 32, 2)

    def second(n, carry):
        for y in range(12):
            pre = acc2[n + 3, y + 2]
            spre_o[n, y] = pre
            fine[n, y] = silu(pre).astype(BF)
        return carry

    lax.fori_loop(0, 6, second, 0)

    def passed(n, carry):
        for y in range(10):
            fpre_o[n, y] = acc1[n + 4, y + 3]
            t1_o[n, y] = t1[n + 3, y + 3]
            t2_o[n, y] = t2[n + 3, y + 3]
        return carry

    lax.fori_loop(0, 4, passed, 0)
    for x in range(2):
        for y in range(8):
            whole = pltpu.roll(fine[x + 2, y + 2].astype(F32), LANES - 8, 1)
            skip_o[x, y] = whole[:, :128].astype(BF)

    matrix = pool[...]
    for x in range(3):
        for y in range(6):
            cube = fine[2 * x : 2 * x + 2, 2 * y : 2 * y + 2].reshape(128, LANES)
            parts = dot(cube, matrix)
            mean = (parts[0:32] + parts[32:64] + parts[64:96] + parts[96:128]) * 0.125
            mean = keep(mean, coarse_ok, (ox // 2 + x - 1, nx // 2), (oy // 2 + y - 1, ny // 2))
            store_taps(t3, (x, y), mean.astype(BF).astype(F32))

    own = lane_mask(128, 0, 4, 68)
    raw = [jnp.zeros((64, 288), F32) for _ in range(3)]
    for y in range(4):
        pre = jnp.zeros((64, 128), F32)
        for i in range(3):
            pre = pre + dot(w3[i], rows_at(t3, i, y + 1))
        coarse_o[y] = silu(pre).astype(BF)
        grad = cot[y].astype(F32) * slope(pre)
        cgrad_o[y] = grad.astype(BF)
        mine = jnp.where(own > 0.5, grad, 0.0).astype(BF)
        for i in range(3):
            raw[i] = raw[i] + dot_lanes(mine, rows_at(t3, i, y + 1))
    for i in range(3):
        craw_o[i * 64 : (i + 1) * 64] = raw[i]


def second_kernel(
    sizes, offs, cgrad, spre, cot, t2, w3, spread, t5, sraw_o, t4, acc4, own5
):
    nx, ny, nz = sizes
    ox, oy, oz = offs[0], offs[1], offs[2]
    fine_ok = lane_mask(LANES, oz - 8, 0, nz)
    own_ok = lane_mask(LANES, 0, 8, 136)

    for x in range(5):
        for y in range(8):
            store_taps(t4, (x, y), cgrad[x, y].astype(F32))
    spread_conv(acc4, w3, t4, (0, 5), (1, 7), 32, 2)
    for x in (0, 1, 4, 5):
        own5[x] = jnp.zeros(own5.shape[1:], BF)
    matrix = spread[...]

    def second(n, carry):
        for cy in range(6):
            value = acc4[n + 2, cy + 1]
            high = value.astype(BF)
            low = (value - high.astype(F32)).astype(BF)
            wide = dot(high, matrix) + dot(low, matrix)
            for dx in range(2):
                for dy in range(2):
                    x, y = 2 * n + dx, 2 * cy + dy
                    grad = (cot[x, y].astype(F32) + wide) * slope(spre[x, y])
                    grad = keep(grad, fine_ok, (ox + x - 2, nx), (oy + y - 2, ny))
                    store_taps(t5, (x, y), grad.astype(BF).astype(F32))
        return carry

    lax.fori_loop(0, 3, second, 0)
    for x in range(2):
        for y in range(8):
            mine = t5[x + 2, y + 2, 32:64].astype(F32)
            own5[x + 2, y] = jnp.where(own_ok > 0.5, mine, 0.0).astype(BF)
    weight_sums(sraw_o, own5, t2)


def weight_sums(out, own, tapped):
    out[...] = jnp.zeros(out.shape, F32)

    def one(n, carry):
        total = jnp.zeros(out.shape, F32)
        for y in range(8):
            left = jnp.concatenate([own[n + 2, y], own[n + 1, y], own[n, y]], axis=0)
            total = total + dot_lanes(left, rows_at(tapped, n, y + 1))
        out[...] += total
        return carry

    lax.fori_loop(0, 4, one, 0)


def first_kernel(sizes, offs, t5, fpre, t1, w2, w1, vgrad_o, fraw_o, acc5, t6, own6):
    nx, ny, nz = sizes
    ox, oy, oz = offs[0], offs[1], offs[2]
    fine_ok = lane_mask(LANES, oz - 8, 0, nz)
    own_ok = lane_mask(LANES, 0, 8, 136)
    for x in (0, 1, 4, 5):
        own6[x] = jnp.zeros(own6.shape[1:], BF)
    spread_conv(acc5, w2, t5, (0, 6), (1, 11), 32, 2)

    def first(n, carry):
        for y in range(10):
            grad = acc5[n + 2, y + 1] * slope(fpre[n, y])
            grad = keep(grad, fine_ok, (ox + n - 1, nx), (oy + y - 1, ny))
            store_taps(t6, (n, y), grad.astype(BF).astype(F32))
        return carry

    lax.fori_loop(0, 4, first, 0)
    for x in range(2):
        for y in range(8):
            mine = t6[x + 1, y + 1, 32:64].astype(F32)
            own6[x + 2, y] = jnp.where(own_ok > 0.5, mine, 0.0).astype(BF)
    weight_sums(fraw_o, own6, t1)
    for x in range(2):
        for y in range(8):
            total = jnp.zeros((16, LANES), F32)
            for i in range(3):
                total = total + dot(w1[i], rows_at(t6, x + i, y + 1))
            vgrad_o[x, y] = pltpu.roll(total, LANES - 8, 1)[:, :128].astype(BF)


def flipped(weight):
    return jnp.transpose(weight[:, ::-1, ::-1, ::-1, :], (4, 1, 2, 3, 0))


def stacked(weight):
    outputs, chans = weight.shape[0], weight.shape[4]
    return jnp.transpose(weight, (1, 0, 2, 3, 4)).reshape(3, outputs, 9 * chans)


def swap(blocks, axes):
    return lax.all_to_all(blocks, axes, split_axis=0, concat_axis=0, tiled=True)


def added(blocks):
    return lax.optimization_barrier(jnp.sum(blocks.astype(F32), axis=0)).astype(BF)


def spread_rows(coarse_raw, second_raw):
    wide = jnp.concatenate([coarse_raw, second_raw], axis=0).astype(BF)
    piece = wide.shape[0] // 4
    rest = [wide[n * piece : (n + 1) * piece, 256:288] for n in range(4)]
    return jnp.concatenate(
        [wide[:, :128], wide[:, 128:256], jnp.concatenate(rest, axis=1)], axis=0
    )


def gathered_rows(rows):
    height, piece = 288, 72
    rest = rows[2 * height : 2 * height + piece]
    rest = jnp.concatenate([rest[:, 32 * n : 32 * n + 32] for n in range(4)], axis=0)
    wide = jnp.concatenate([rows[:height], rows[height : 2 * height], rest], axis=1)
    return wide[192:], wide[:192]


def plane_blocks(blocks):
    count = lax.axis_size("gy")
    place = lax.broadcasted_iota(jnp.int32, (count, 1, 1, 1), 0)
    mine = jnp.where(place == lax.axis_index("gy"), blocks[None], jnp.zeros((), blocks.dtype))
    return mine.reshape((count * blocks.shape[0],) + blocks.shape[1:])


def total_over_line(part):
    count = lax.axis_size("gx")
    other = lax.ppermute(part, "gx", [(i, i ^ 1) for i in range(count)])
    part = added(jnp.stack([part, other]))
    groups = [list(range(n, count, 2)) for n in range(2)]
    sent = jnp.broadcast_to(part, (count // 2,) + part.shape)
    return added(
        lax.all_to_all(
            sent, "gx", split_axis=0, concat_axis=0, tiled=True, axis_index_groups=groups
        )
    )


def weight_form(matrix, outputs, chans):
    return jnp.transpose(matrix.reshape(3, outputs, 3, 3, chans), (1, 0, 2, 3, 4))


def shape(dims, dtype):
    return jax.ShapeDtypeStruct(dims, dtype)


def local(volume, w_first, w_second, w_coarse, skip_cotangent, coarse_cotangent):
    counts = [lax.axis_size(axis) for axis in AXES]
    extents = volume.shape[1:]
    sizes = tuple(count * extent for count, extent in zip(counts, extents))
    offs = jnp.stack([lax.axis_index(axis) * extent for axis, extent in zip(AXES, extents)])
    offs = offs.astype(jnp.int32)

    line_volume = halo(volume, "gx", 1, 4)
    wide_volume = halo(halo(line_volume, "gy", 2, 4), "gz", 3, 8)
    wide_volume = jnp.pad(
        jnp.transpose(wide_volume, (1, 2, 0, 3)), ((0, 0), (0, 0), (0, 12), (0, LANES - 144))
    )
    sides = counts[2]
    depth = coarse_cotangent.shape[3] // sides
    guarded = jnp.pad(coarse_cotangent[:, 0], ((0, 0), (0, 0), (2, 2)))
    sent = jnp.stack([guarded[..., n * depth : n * depth + depth + 4] for n in range(sides)])
    returned = swap(sent, "gz")
    returned = jnp.transpose(returned, (2, 0, 1, 3)).reshape(4, 64, depth + 4)
    returned = jnp.pad(returned, ((0, 0), (0, 0), (2, 128 - 70)))
    later = line_volume[0, 0, 0, 0] * 0 + line_volume[0, 9, 0, 0] * 0
    rows_cotangent = jnp.transpose(skip_cotangent, (1, 2, 0, 3)) + later
    wide_cotangent = halo(halo(halo(rows_cotangent, "gx", 0, 2), "gy", 1, 2), "gz", 3, 2)
    wide_cotangent = jnp.pad(wide_cotangent, ((0, 0), (0, 0), (0, 0), (6, LANES - 138)))

    fine_place = lax.broadcasted_iota(jnp.int32, (LANES, 128), 0)
    coarse_place = lax.broadcasted_iota(jnp.int32, (LANES, 128), 1)
    pool = jnp.where(fine_place // 2 == coarse_place, 1.0, 0.0).astype(BF)
    spread = jnp.transpose(pool) * 0.125

    thin_first = jnp.pad(w_first, ((0, 0), (0, 0), (0, 0), (0, 0), (0, 12)))
    smem = pl.BlockSpec(memory_space=pltpu.SMEM)
    vmem = pl.BlockSpec(memory_space=pltpu.VMEM)
    skip, coarse_local, coarse_grad, coarse_raw, first_pre, second_pre, taps1, taps2 = (
        pl.pallas_call(
            lambda *refs: forward_kernel(sizes, *refs),
            out_shape=(
                shape((2, 8, 32, 128), BF),
                shape((4, 64, 128), BF),
                shape((4, 64, 128), BF),
                shape((192, 288), F32),
                shape((4, 10, 32, LANES), F32),
                shape((6, 12, 32, LANES), F32),
                shape((4, 10, 48, LANES), BF),
                shape((4, 10, 96, LANES), BF),
            ),
            in_specs=[smem] + [vmem] * 6 + [pl.BlockSpec(memory_space=pl.ANY)],
            out_specs=(vmem,) * 8,
            scratch_shapes=[
                pltpu.VMEM((10, 16, 48, LANES), BF),
                pltpu.VMEM((12, 16, 32, LANES), F32),
                pltpu.VMEM((10, 16, 96, LANES), BF),
                pltpu.VMEM((12, 16, 32, LANES), F32),
                pltpu.VMEM((6, 12, 32, LANES), BF),
                pltpu.VMEM((3, 6, 96, 128), BF),
            ],
            compiler_params=pltpu.CompilerParams(vmem_limit_bytes=52 * 2**20),
            cost_estimate=pl.CostEstimate(
                flops=4 * 10**9, bytes_accessed=12 * 10**6, transcendentals=10**6
            ),
            name="forward",
        )(
            offs,
            wide_volume,
            stacked(thin_first).reshape(96, 144),
            stacked(w_second).reshape(96, 288),
            stacked(w_coarse),
            returned,
            pool,
            wide_cotangent,
        )
    )
    wide_grad = halo(halo(coarse_grad[None], "gx", 0, 2), "gy", 1, 2)
    taps5, second_raw = pl.pallas_call(
        lambda *refs: second_kernel(sizes, *refs),
        out_shape=(shape((6, 12, 96, LANES), BF), shape((96, 288), F32)),
        in_specs=[smem] + [vmem] * 6,
        out_specs=(vmem,) * 2,
        scratch_shapes=[
            pltpu.VMEM((5, 8, 192, 128), BF),
            pltpu.VMEM((7, 8, 32, 128), F32),
            pltpu.VMEM((6, 8, 32, LANES), BF),
        ],
        compiler_params=pltpu.CompilerParams(vmem_limit_bytes=48 * 2**20),
        cost_estimate=pl.CostEstimate(
            flops=10**9, bytes_accessed=10 * 10**6, transcendentals=10**6
        ),
        name="second",
    )(
        offs,
        wide_grad,
        second_pre,
        wide_cotangent,
        taps2,
        stacked(flipped(w_coarse)).reshape(96, 576),
        spread,
    )

    plane = ("gy", "gz")
    count = counts[1] * counts[2]
    rows = spread_rows(coarse_raw, second_raw)
    share = -(-rows.shape[0] // (8 * count)) * 8
    rows = jnp.pad(rows, ((0, share * count - rows.shape[0]), (0, 0)))
    blocks = coarse_local[:, :, 4 : 4 + depth].reshape(4, sides, 64 // sides, depth)
    blocks = jnp.transpose(blocks, (1, 0, 2, 3)).reshape(sides, -1, depth)
    half = blocks.shape[1] // 2
    blocks = jnp.concatenate([blocks[:, :half], blocks[:, half:]], axis=2)
    arrived = swap(
        jnp.concatenate([rows.reshape(count, share, 128), plane_blocks(blocks)], axis=1), plane
    )

    back_first = jnp.pad(flipped(w_first), ((0, 12),) + ((0, 0),) * 4)
    volume_grad, first_raw = pl.pallas_call(
        lambda *refs: first_kernel(sizes, *refs),
        out_shape=(shape((2, 8, 16, 128), BF), shape((96, 144), F32)),
        in_specs=[smem] + [vmem] * 5,
        out_specs=(vmem,) * 2,
        scratch_shapes=[
            pltpu.VMEM((8, 12, 32, LANES), F32),
            pltpu.VMEM((4, 10, 96, LANES), BF),
            pltpu.VMEM((6, 8, 32, LANES), BF),
        ],
        compiler_params=pltpu.CompilerParams(vmem_limit_bytes=48 * 2**20),
        cost_estimate=pl.CostEstimate(
            flops=2 * 10**9, bytes_accessed=10 * 10**6, transcendentals=10**6
        ),
        name="first",
    )(
        offs,
        taps5,
        first_pre,
        taps1,
        stacked(flipped(w_second)).reshape(96, 288),
        stacked(back_first),
    )

    part = added(arrived[:, :share])
    own_row = lax.axis_index("gy") * sides
    coarse = lax.dynamic_slice_in_dim(arrived[:, share:], own_row, sides, axis=0)
    coarse = jnp.concatenate([coarse[:, :, :depth], coarse[:, :, depth:]], axis=1)
    coarse = coarse.reshape(sides, 4, 64 // sides, depth)
    coarse = jnp.transpose(coarse, (2, 1, 0, 3)).reshape(64 // sides, 1, 4, sides * depth)

    thin = first_raw.reshape(3, 32, 9, 16)[..., :4].reshape(3, 32, 36).astype(BF)
    thin = jnp.pad(jnp.concatenate([thin[0], thin[1], thin[2]], axis=1), ((0, 0), (0, 20)))
    part = total_over_line(jnp.concatenate([part, thin], axis=0))
    whole = swap(jnp.broadcast_to(part, (count,) + part.shape), plane)
    second, wide = gathered_rows(whole[:, :share].reshape(count * share, 128).astype(F32))
    thin = jnp.sum(whole[:, share:].astype(F32), axis=0)
    thin = jnp.stack([thin[:, 36 * n : 36 * n + 36] for n in range(3)])

    skip = jnp.transpose(skip, (2, 0, 1, 3))
    volume_grad = jnp.transpose(volume_grad[:, :, :4], (2, 0, 1, 3))
    factor = 1.0 / math.sqrt(sizes[0] * sizes[1] * sizes[2])
    return (
        skip,
        coarse,
        volume_grad,
        weight_form(thin * factor, 32, 4),
        weight_form(second * factor, 32, 32),
        weight_form(wide * factor, 64, 32),
    )


def solution(mesh):
    in_specs = (
        P(None, "gx", "gy", "gz"),
        P(),
        P(),
        P(),
        P(None, "gx", "gy", "gz"),
        P("gz", "gx", "gy", None),
    )
    out_specs = (
        P(None, "gx", "gy", "gz"),
        P("gz", "gx", "gy", None),
        P(None, "gx", "gy", "gz"),
        P(),
        P(),
        P(),
    )
    return jax.shard_map(local, mesh=mesh, in_specs=in_specs, out_specs=out_specs, check_vma=False)
```

```python
import math

import jax
import jax.numpy as jnp
from jax import lax
from jax.experimental import pallas as pl
from jax.experimental.pallas import tpu as pltpu
from jax.sharding import PartitionSpec as P

AXES = ("gx", "gy", "gz")
LANES = 256
BF = jnp.bfloat16
F32 = jnp.float32


def shifted(block, axis, step):
    count = lax.axis_size(axis)
    pairs = [(i, i + step) for i in range(count) if 0 <= i + step < count]
    return lax.ppermute(block, axis, pairs)


def halo(cells, axis, dim, width):
    extent = cells.shape[dim]
    before, after = [], []
    for step in range(1, -(-width // extent) + 1):
        part = min(extent, width - (step - 1) * extent)
        tail = lax.slice_in_dim(cells, extent - part, extent, axis=dim)
        head = lax.slice_in_dim(cells, 0, part, axis=dim)
        before.insert(0, shifted(tail, axis, step))
        after.append(shifted(head, axis, -step))
    return jnp.concatenate(before + [cells] + after, axis=dim)


def slope(values):
    sigmoid_value = jax.nn.sigmoid(values)
    return sigmoid_value * (1.0 + values * (1.0 - sigmoid_value))


def silu(values):
    return values * jax.nn.sigmoid(values)


def store_taps(ref, place, values):
    chans, lanes = values.shape
    ref[place + (slice(0, chans),)] = pltpu.roll(values, 1, 1).astype(BF)
    ref[place + (slice(chans, 2 * chans),)] = values.astype(BF)
    ref[place + (slice(2 * chans, 3 * chans),)] = pltpu.roll(values, lanes - 1, 1).astype(BF)


def rows_at(ref, plane, row):
    part = ref[plane, row - 1 : row + 2]
    return part.reshape(part.shape[0] * part.shape[1], part.shape[2])


def dot(left, right):
    return jnp.dot(left, right, preferred_element_type=F32)


def dot_lanes(left, right):
    return lax.dot_general(left, right, (((1,), (1,)), ((), ())), preferred_element_type=F32)


def lane_mask(lanes, first, low, high):
    place = first + lax.broadcasted_iota(jnp.int32, (1, lanes), 1)
    return jnp.where((place >= low) & (place < high), 1.0, 0.0).astype(F32)


def keep(values, lanes_ok, *bounds):
    good = None
    for place, limit in bounds:
        here = (place >= 0) & (place < limit)
        good = here if good is None else good & here
    mask = lanes_ok * jnp.where(good, 1.0, 0.0).astype(F32)
    return jnp.where(mask > 0.5, values, 0.0)


def spread_conv(acc, weights, tapped, planes, rows, outputs, shift):
    matrix = weights[...]

    def one(n, carry):
        plane = planes[0] + n
        for row in range(*rows):
            summed = dot(matrix, rows_at(tapped, plane, row))
            acc[plane + shift, row] = summed[:outputs]
            for i in (1, 2):
                place = plane + shift - i
                acc[place, row] = acc[place, row] + summed[i * outputs : (i + 1) * outputs]
        return carry

    lax.fori_loop(0, planes[1] - planes[0], one, 0)


def forward_kernel(
    sizes, offs, vol, w1, w2, w3, cot, pool, unread_a, unread_b,
    skip_o, coarse_o, cgrad_o, craw_o, fpre_o, spre_o, t1_o, t2_o,
    t1, acc1, t2, acc2, fine, t3,
):
    nx, ny, nz = sizes
    ox, oy, oz = offs[0], offs[1], offs[2]
    fine_ok = lane_mask(LANES, oz - 8, 0, nz)
    coarse_ok = lane_mask(128, oz // 2 - 4, 0, nz // 2)

    def volume_taps(x, carry):
        for y in range(16):
            here = vol[x, y].astype(F32)
            moved = [pltpu.roll(here, 1, 1), here, pltpu.roll(here, LANES - 1, 1)]
            t1[x, y] = jnp.concatenate(moved + [jnp.zeros_like(here)], axis=0).astype(BF)
        return carry

    lax.fori_loop(0, 10, volume_taps, 0)
    spread_conv(acc1, w1, t1, (0, 10), (1, 15), 32, 2)

    def first(n, carry):
        x = n + 1
        for y in range(1, 15):
            act = silu(acc1[x + 1, y])
            act = keep(act, fine_ok, (ox + x - 4, nx), (oy + y - 4, ny))
            store_taps(t2, (x, y), act.astype(BF).astype(F32))
        return carry

    lax.fori_loop(0, 8, first, 0)
    spread_conv(acc2, w2, t2, (1, 9), (2, 14), 32, 2)

    def second(n, carry):
        for y in range(12):
            pre = acc2[n + 3, y + 2]
            spre_o[n, y] = pre
            fine[n, y] = silu(pre).astype(BF)
        return carry

    lax.fori_loop(0, 6, second, 0)

    def passed(n, carry):
        for y in range(10):
            fpre_o[n, y] = acc1[n + 4, y + 3]
            t1_o[n, y] = t1[n + 3, y + 3]
            t2_o[n, y] = t2[n + 3, y + 3]
        return carry

    lax.fori_loop(0, 4, passed, 0)
    for x in range(2):
        for y in range(8):
            whole = pltpu.roll(fine[x + 2, y + 2].astype(F32), LANES - 8, 1)
            skip_o[x, y] = whole[:, :128].astype(BF)

    matrix = pool[...]
    for x in range(3):
        for y in range(6):
            cube = fine[2 * x : 2 * x + 2, 2 * y : 2 * y + 2].reshape(128, LANES)
            parts = dot(cube, matrix)
            mean = (parts[0:32] + parts[32:64] + parts[64:96] + parts[96:128]) * 0.125
            mean = keep(mean, coarse_ok, (ox // 2 + x - 1, nx // 2), (oy // 2 + y - 1, ny // 2))
            store_taps(t3, (x, y), mean.astype(BF).astype(F32))

    own = lane_mask(128, 0, 4, 68)
    raw = [jnp.zeros((64, 288), F32) for _ in range(3)]
    for y in range(4):
        pre = jnp.zeros((64, 128), F32)
        for i in range(3):
            pre = pre + dot(w3[i], rows_at(t3, i, y + 1))
        coarse_o[y] = silu(pre).astype(BF)
        grad = cot[y].astype(F32) * slope(pre)
        cgrad_o[y] = grad.astype(BF)
        mine = jnp.where(own > 0.5, grad, 0.0).astype(BF)
        for i in range(3):
            raw[i] = raw[i] + dot_lanes(mine, rows_at(t3, i, y + 1))
    for i in range(3):
        craw_o[i * 64 : (i + 1) * 64] = raw[i]


def second_kernel(
    sizes, offs, cgrad, spre, cot, t2, w3, spread, t5, sraw_o, t4, acc4, own5
):
    nx, ny, nz = sizes
    ox, oy, oz = offs[0], offs[1], offs[2]
    fine_ok = lane_mask(LANES, oz - 8, 0, nz)
    own_ok = lane_mask(LANES, 0, 8, 136)

    for x in range(5):
        for y in range(8):
            store_taps(t4, (x, y), cgrad[x, y].astype(F32))
    spread_conv(acc4, w3, t4, (0, 5), (1, 7), 32, 2)
    for x in (0, 1, 4, 5):
        own5[x] = jnp.zeros(own5.shape[1:], BF)
    matrix = spread[...]

    def second(n, carry):
        for cy in range(6):
            value = acc4[n + 2, cy + 1]
            high = value.astype(BF)
            low = (value - high.astype(F32)).astype(BF)
            wide = dot(high, matrix) + dot(low, matrix)
            for dx in range(2):
                for dy in range(2):
                    x, y = 2 * n + dx, 2 * cy + dy
                    grad = (cot[x, y].astype(F32) + wide) * slope(spre[x, y])
                    grad = keep(grad, fine_ok, (ox + x - 2, nx), (oy + y - 2, ny))
                    store_taps(t5, (x, y), grad.astype(BF).astype(F32))
        return carry

    lax.fori_loop(0, 3, second, 0)
    for x in range(2):
        for y in range(8):
            mine = t5[x + 2, y + 2, 32:64].astype(F32)
            own5[x + 2, y] = jnp.where(own_ok > 0.5, mine, 0.0).astype(BF)
    weight_sums(sraw_o, own5, t2)


def weight_sums(out, own, tapped):
    out[...] = jnp.zeros(out.shape, F32)

    def one(n, carry):
        total = jnp.zeros(out.shape, F32)
        for y in range(8):
            left = jnp.concatenate([own[n + 2, y], own[n + 1, y], own[n, y]], axis=0)
            total = total + dot_lanes(left, rows_at(tapped, n, y + 1))
        out[...] += total
        return carry

    lax.fori_loop(0, 4, one, 0)


def first_kernel(sizes, offs, t5, fpre, t1, w2, t6, thin_o, acc5, own6, fraw):
    nx, ny, nz = sizes
    ox, oy, oz = offs[0], offs[1], offs[2]
    fine_ok = lane_mask(LANES, oz - 8, 0, nz)
    own_ok = lane_mask(LANES, 0, 8, 136)
    for x in (0, 1, 4, 5):
        own6[x] = jnp.zeros(own6.shape[1:], BF)
    spread_conv(acc5, w2, t5, (0, 6), (1, 11), 32, 2)

    def first(n, carry):
        for y in range(10):
            grad = acc5[n + 2, y + 1] * slope(fpre[n, y])
            grad = keep(grad, fine_ok, (ox + n - 1, nx), (oy + y - 1, ny))
            store_taps(t6, (n, y), grad.astype(BF).astype(F32))
        return carry

    lax.fori_loop(0, 4, first, 0)
    for x in range(2):
        for y in range(8):
            mine = t6[x + 1, y + 1, 32:64].astype(F32)
            own6[x + 2, y] = jnp.where(own_ok > 0.5, mine, 0.0).astype(BF)
    weight_sums(fraw, own6, t1)
    place = lax.broadcasted_iota(jnp.int32, (48, 128), 0)
    lane = lax.broadcasted_iota(jnp.int32, (48, 128), 1)
    term = place & 15
    column = jnp.where(term < 12, (place >> 4) * 12 + term, -200)
    thin = jnp.zeros((32, 128), F32)
    for i in range(3):
        picked = jnp.where(lane == column + 36 * i, 1.0, 0.0).astype(BF)
        thin = thin + dot(fraw[32 * i : 32 * i + 32].astype(BF), picked)
    thin_o[...] = thin.astype(BF)


def volume_kernel(t6, w1, vgrad_o):
    for x in range(2):
        for y in range(8):
            total = jnp.zeros((16, LANES), F32)
            for i in range(3):
                total = total + dot(w1[i], rows_at(t6, x + i, y + 1))
            vgrad_o[x, y] = pltpu.roll(total, LANES - 8, 1)[:, :128].astype(BF)


def flipped(weight):
    return jnp.transpose(weight[:, ::-1, ::-1, ::-1, :], (4, 1, 2, 3, 0))


def stacked(weight):
    outputs, chans = weight.shape[0], weight.shape[4]
    return jnp.transpose(weight, (1, 0, 2, 3, 4)).reshape(3, outputs, 9 * chans)


def swap(blocks, axes):
    return lax.all_to_all(blocks, axes, split_axis=0, concat_axis=0, tiled=True)


def added(blocks):
    return lax.optimization_barrier(jnp.sum(blocks.astype(F32), axis=0)).astype(BF)


def spread_rows(coarse_raw, second_raw):
    wide = jnp.concatenate([coarse_raw, second_raw], axis=0).astype(BF)
    piece = wide.shape[0] // 4
    rest = [wide[n * piece : (n + 1) * piece, 256:288] for n in range(4)]
    return jnp.concatenate(
        [wide[:, :128], wide[:, 128:256], jnp.concatenate(rest, axis=1)], axis=0
    )


def gathered_rows(rows):
    height, piece = 288, 72
    rest = rows[2 * height : 2 * height + piece]
    rest = jnp.concatenate([rest[:, 32 * n : 32 * n + 32] for n in range(4)], axis=0)
    wide = jnp.concatenate([rows[:height], rows[height : 2 * height], rest], axis=1)
    return wide[192:], wide[:192]


def plane_blocks(blocks):
    count = lax.axis_size("gy")
    place = lax.broadcasted_iota(jnp.int32, (count, 1, 1, 1), 0)
    mine = jnp.where(place == lax.axis_index("gy"), blocks[None], jnp.zeros((), blocks.dtype))
    return mine.reshape((count * blocks.shape[0],) + blocks.shape[1:])


def weight_form(matrix, outputs, chans):
    return jnp.transpose(matrix.reshape(3, outputs, 3, 3, chans), (1, 0, 2, 3, 4))


def shape(dims, dtype):
    return jax.ShapeDtypeStruct(dims, dtype)


def local(volume, w_first, w_second, w_coarse, skip_cotangent, coarse_cotangent):
    counts = [lax.axis_size(axis) for axis in AXES]
    extents = volume.shape[1:]
    sizes = tuple(count * extent for count, extent in zip(counts, extents))
    offs = jnp.stack([lax.axis_index(axis) * extent for axis, extent in zip(AXES, extents)])
    offs = offs.astype(jnp.int32)

    rows_volume = jnp.transpose(volume, (1, 2, 0, 3))
    rows_cotangent = jnp.transpose(skip_cotangent, (1, 2, 0, 3))
    both = jnp.concatenate([rows_cotangent, rows_volume], axis=2)
    chans = skip_cotangent.shape[0]
    near = (shifted(both, "gx", 1), shifted(both, "gx", -1))
    far = (shifted(rows_volume, "gx", 2), shifted(rows_volume, "gx", -2))
    wide_volume = jnp.concatenate(
        [far[0], near[0][:, :, chans:], rows_volume, near[1][:, :, chans:], far[1]], axis=0
    )
    wide_volume = halo(halo(wide_volume, "gy", 1, 4), "gz", 3, 8)
    wide_volume = jnp.pad(wide_volume, ((0, 0), (0, 0), (0, 0), (0, LANES - 144)))
    tall_cotangent = jnp.concatenate(
        [near[0][:, :, :chans], rows_cotangent, near[1][:, :, :chans]], axis=0
    )
    tall_cotangent = halo(tall_cotangent, "gy", 1, 2)
    edges = (
        shifted(tall_cotangent[..., -2:], "gz", 1),
        shifted(tall_cotangent[..., :2], "gz", -1),
    )
    wide_cotangent = jnp.concatenate([edges[0], tall_cotangent, edges[1]], axis=3)
    wide_cotangent = jnp.pad(wide_cotangent, ((0, 0), (0, 0), (0, 0), (6, LANES - 138)))
    sides = counts[2]
    depth = coarse_cotangent.shape[3] // sides
    guarded = jnp.pad(coarse_cotangent[:, 0], ((0, 0), (0, 0), (2, 2)))
    sent = jnp.stack([guarded[..., n * depth : n * depth + depth + 4] for n in range(sides)])
    returned = swap(sent, "gz")
    returned = jnp.transpose(returned, (2, 0, 1, 3)).reshape(4, 64, depth + 4)
    returned = jnp.pad(returned, ((0, 0), (0, 0), (2, 128 - 70)))
    fine_place = lax.broadcasted_iota(jnp.int32, (LANES, 128), 0)
    coarse_place = lax.broadcasted_iota(jnp.int32, (LANES, 128), 1)
    pool = jnp.where(fine_place // 2 == coarse_place, 1.0, 0.0).astype(BF)
    spread = jnp.transpose(pool) * 0.125

    thin_first = jnp.transpose(w_first, (1, 0, 2, 3, 4)).reshape(96, 3, 12)
    thin_first = jnp.pad(thin_first, ((0, 0), (0, 0), (0, 4))).reshape(96, 48)
    smem = pl.BlockSpec(memory_space=pltpu.SMEM)
    vmem = pl.BlockSpec(memory_space=pltpu.VMEM)
    skip, coarse_local, coarse_grad, coarse_raw, first_pre, second_pre, taps1, taps2 = (
        pl.pallas_call(
            lambda *refs: forward_kernel(sizes, *refs),
            out_shape=(
                shape((2, 8, 32, 128), BF),
                shape((4, 64, 128), BF),
                shape((4, 64, 128), BF),
                shape((192, 288), F32),
                shape((4, 10, 32, LANES), F32),
                shape((6, 12, 32, LANES), F32),
                shape((4, 10, 16, LANES), BF),
                shape((4, 10, 96, LANES), BF),
            ),
            in_specs=[smem] + [vmem] * 6 + [pl.BlockSpec(memory_space=pl.ANY)] * 2,
            out_specs=(vmem,) * 8,
            scratch_shapes=[
                pltpu.VMEM((10, 16, 16, LANES), BF),
                pltpu.VMEM((12, 16, 32, LANES), F32),
                pltpu.VMEM((10, 16, 96, LANES), BF),
                pltpu.VMEM((12, 16, 32, LANES), F32),
                pltpu.VMEM((6, 12, 32, LANES), BF),
                pltpu.VMEM((3, 6, 96, 128), BF),
            ],
            compiler_params=pltpu.CompilerParams(vmem_limit_bytes=52 * 2**20),
            cost_estimate=pl.CostEstimate(
                flops=4 * 10**9, bytes_accessed=12 * 10**6, transcendentals=10**6
            ),
            name="forward",
        )(
            offs,
            wide_volume,
            thin_first,
            stacked(w_second).reshape(96, 288),
            stacked(w_coarse),
            returned,
            pool,
            *edges,
        )
    )
    wide_grad = halo(halo(coarse_grad[None], "gx", 0, 2), "gy", 1, 2)
    taps5, second_raw = pl.pallas_call(
        lambda *refs: second_kernel(sizes, *refs),
        out_shape=(shape((6, 12, 96, LANES), BF), shape((96, 288), F32)),
        in_specs=[smem] + [vmem] * 6,
        out_specs=(vmem,) * 2,
        scratch_shapes=[
            pltpu.VMEM((5, 8, 192, 128), BF),
            pltpu.VMEM((7, 8, 32, 128), F32),
            pltpu.VMEM((6, 8, 32, LANES), BF),
        ],
        compiler_params=pltpu.CompilerParams(vmem_limit_bytes=48 * 2**20),
        cost_estimate=pl.CostEstimate(
            flops=10**9, bytes_accessed=10 * 10**6, transcendentals=10**6
        ),
        name="second",
    )(
        offs,
        wide_grad,
        second_pre,
        wide_cotangent,
        taps2,
        stacked(flipped(w_coarse)).reshape(96, 576),
        spread,
    )

    plane = ("gy", "gz")
    count = counts[1] * counts[2]
    rows = spread_rows(coarse_raw, second_raw)
    share = -(-rows.shape[0] // (8 * count)) * 8
    rows = jnp.pad(rows, ((0, share * count - rows.shape[0]), (0, 0)))
    blocks = coarse_local[:, :, 4 : 4 + depth].reshape(4, sides, 64 // sides, depth)
    blocks = jnp.transpose(blocks, (1, 0, 2, 3)).reshape(sides, -1, depth)
    half = blocks.shape[1] // 2
    blocks = jnp.concatenate([blocks[:, :half], blocks[:, half:]], axis=2)
    arrived = swap(
        jnp.concatenate([rows.reshape(count, share, 128), plane_blocks(blocks)], axis=1), plane
    )

    taps6, thin = pl.pallas_call(
        lambda *refs: first_kernel(sizes, *refs),
        out_shape=(shape((4, 10, 96, LANES), BF), shape((32, 128), BF)),
        in_specs=[smem] + [vmem] * 4,
        out_specs=(vmem,) * 2,
        scratch_shapes=[
            pltpu.VMEM((8, 12, 32, LANES), F32),
            pltpu.VMEM((6, 8, 32, LANES), BF),
            pltpu.VMEM((96, 48), F32),
        ],
        compiler_params=pltpu.CompilerParams(vmem_limit_bytes=48 * 2**20),
        cost_estimate=pl.CostEstimate(
            flops=2 * 10**9, bytes_accessed=10 * 10**6, transcendentals=10**6
        ),
        name="first",
    )(offs, taps5, first_pre, taps1, stacked(flipped(w_second)).reshape(96, 288))
    back_first = jnp.pad(flipped(w_first), ((0, 12),) + ((0, 0),) * 4)
    volume_grad = pl.pallas_call(
        volume_kernel,
        out_shape=shape((2, 8, 16, 128), BF),
        in_specs=[vmem] * 2,
        out_specs=vmem,
        compiler_params=pltpu.CompilerParams(vmem_limit_bytes=48 * 2**20),
        cost_estimate=pl.CostEstimate(
            flops=10**9, bytes_accessed=4 * 10**6, transcendentals=0
        ),
        name="volume",
    )(taps6, stacked(back_first))

    part = added(arrived[:, :share])
    own_row = lax.axis_index("gy") * sides
    coarse = lax.dynamic_slice_in_dim(arrived[:, share:], own_row, sides, axis=0)
    coarse = jnp.concatenate([coarse[:, :, :depth], coarse[:, :, depth:]], axis=1)
    coarse = coarse.reshape(sides, 4, 64 // sides, depth)
    coarse = jnp.transpose(coarse, (2, 1, 0, 3)).reshape(64 // sides, 1, 4, sides * depth)

    part = jnp.concatenate([part, thin], axis=0)
    part = added(swap(jnp.broadcast_to(part, (counts[0],) + part.shape), "gx"))
    whole = swap(jnp.broadcast_to(part, (count,) + part.shape), plane)
    second, wide = gathered_rows(whole[:, :share].reshape(count * share, 128).astype(F32))
    thin = jnp.sum(whole[:, share:].astype(F32), axis=0)
    thin = jnp.stack([thin[:, 36 * n : 36 * n + 36] for n in range(3)])

    skip = jnp.transpose(skip, (2, 0, 1, 3))
    volume_grad = jnp.transpose(volume_grad[:, :, :4], (2, 0, 1, 3))
    factor = 1.0 / math.sqrt(sizes[0] * sizes[1] * sizes[2])
    return (
        skip,
        coarse,
        volume_grad,
        weight_form(thin * factor, 32, 4),
        weight_form(second * factor, 32, 32),
        weight_form(wide * factor, 64, 32),
    )


def solution(mesh):
    in_specs = (
        P(None, "gx", "gy", "gz"),
        P(),
        P(),
        P(),
        P(None, "gx", "gy", "gz"),
        P("gz", "gx", "gy", None),
    )
    out_specs = (
        P(None, "gx", "gy", "gz"),
        P("gz", "gx", "gy", None),
        P(None, "gx", "gy", "gz"),
        P(),
        P(),
        P(),
    )
    return jax.shard_map(local, mesh=mesh, in_specs=in_specs, out_specs=out_specs, check_vma=False)
```

```python
import math

import jax
import jax.numpy as jnp
from jax import lax
from jax.experimental import pallas as pl
from jax.experimental.pallas import tpu as pltpu
from jax.sharding import PartitionSpec as P

AXES = ("gx", "gy", "gz")
LANES = 256
BF = jnp.bfloat16
F32 = jnp.float32


def shifted(block, axis, step):
    count = lax.axis_size(axis)
    pairs = [(i, i + step) for i in range(count) if 0 <= i + step < count]
    return lax.ppermute(block, axis, pairs)


def halo(cells, axis, dim, width):
    extent = cells.shape[dim]
    before, after = [], []
    for step in range(1, -(-width // extent) + 1):
        part = min(extent, width - (step - 1) * extent)
        tail = lax.slice_in_dim(cells, extent - part, extent, axis=dim)
        head = lax.slice_in_dim(cells, 0, part, axis=dim)
        before.insert(0, shifted(tail, axis, step))
        after.append(shifted(head, axis, -step))
    return jnp.concatenate(before + [cells] + after, axis=dim)


def slope(values):
    sigmoid_value = jax.nn.sigmoid(values)
    return sigmoid_value * (1.0 + values * (1.0 - sigmoid_value))


def silu(values):
    return values * jax.nn.sigmoid(values)


def store_taps(ref, place, values):
    chans, lanes = values.shape
    ref[place + (slice(0, chans),)] = pltpu.roll(values, 1, 1).astype(BF)
    ref[place + (slice(chans, 2 * chans),)] = values.astype(BF)
    ref[place + (slice(2 * chans, 3 * chans),)] = pltpu.roll(values, lanes - 1, 1).astype(BF)


def rows_at(ref, plane, row):
    part = ref[plane, row - 1 : row + 2]
    return part.reshape(part.shape[0] * part.shape[1], part.shape[2])


def dot(left, right):
    return jnp.dot(left, right, preferred_element_type=F32)


def dot_lanes(left, right):
    return lax.dot_general(left, right, (((1,), (1,)), ((), ())), preferred_element_type=F32)


def lane_mask(lanes, first, low, high):
    place = first + lax.broadcasted_iota(jnp.int32, (1, lanes), 1)
    return jnp.where((place >= low) & (place < high), 1.0, 0.0).astype(F32)


def keep(values, lanes_ok, *bounds):
    good = None
    for place, limit in bounds:
        here = (place >= 0) & (place < limit)
        good = here if good is None else good & here
    mask = lanes_ok * jnp.where(good, 1.0, 0.0).astype(F32)
    return jnp.where(mask > 0.5, values, 0.0)


def spread_conv(acc, weights, tapped, planes, rows, outputs, shift):
    matrix = weights[...]

    def one(n, carry):
        plane = planes[0] + n
        for row in range(*rows):
            summed = dot(matrix, rows_at(tapped, plane, row))
            acc[plane + shift, row] = summed[:outputs]
            for i in (1, 2):
                place = plane + shift - i
                acc[place, row] = acc[place, row] + summed[i * outputs : (i + 1) * outputs]
        return carry

    lax.fori_loop(0, planes[1] - planes[0], one, 0)


def forward_kernel(
    sizes, offs, vol, w1, w2, w3, cot, pool, unread_a, unread_b,
    skip_o, coarse_o, cgrad_o, t3, fpre_o, spre_o, t1_o, t2_o,
    t1, acc1, t2, acc2, fine,
):
    nx, ny, nz = sizes
    ox, oy, oz = offs[0], offs[1], offs[2]
    fine_ok = lane_mask(LANES, oz - 8, 0, nz)
    coarse_ok = lane_mask(128, oz // 2 - 4, 0, nz // 2)

    def volume_taps(x, carry):
        for y in range(16):
            here = vol[x, y].astype(F32)
            moved = [pltpu.roll(here, 1, 1), here, pltpu.roll(here, LANES - 1, 1)]
            t1[x, y] = jnp.concatenate(moved + [jnp.zeros_like(here)], axis=0).astype(BF)
        return carry

    lax.fori_loop(0, 10, volume_taps, 0)
    spread_conv(acc1, w1, t1, (0, 10), (1, 15), 32, 2)

    def first(n, carry):
        x = n + 1
        for y in range(1, 15):
            act = silu(acc1[x + 1, y])
            act = keep(act, fine_ok, (ox + x - 4, nx), (oy + y - 4, ny))
            store_taps(t2, (x, y), act.astype(BF).astype(F32))
        return carry

    lax.fori_loop(0, 8, first, 0)
    spread_conv(acc2, w2, t2, (1, 9), (2, 14), 32, 2)

    def second(n, carry):
        for y in range(12):
            pre = acc2[n + 3, y + 2]
            spre_o[n, y] = pre
            fine[n, y] = silu(pre).astype(BF)
        return carry

    lax.fori_loop(0, 6, second, 0)

    def passed(n, carry):
        for y in range(10):
            fpre_o[n, y] = acc1[n + 4, y + 3]
            t1_o[n, y] = t1[n + 3, y + 3]
            t2_o[n, y] = t2[n + 3, y + 3]
        return carry

    lax.fori_loop(0, 4, passed, 0)
    for x in range(2):
        for y in range(8):
            whole = pltpu.roll(fine[x + 2, y + 2].astype(F32), LANES - 8, 1)
            skip_o[x, y] = whole[:, :128].astype(BF)

    matrix = pool[...]
    for x in range(3):
        for y in range(6):
            cube = fine[2 * x : 2 * x + 2, 2 * y : 2 * y + 2].reshape(128, LANES)
            parts = dot(cube, matrix)
            mean = (parts[0:32] + parts[32:64] + parts[64:96] + parts[96:128]) * 0.125
            mean = keep(mean, coarse_ok, (ox // 2 + x - 1, nx // 2), (oy // 2 + y - 1, ny // 2))
            store_taps(t3, (x, y), mean.astype(BF).astype(F32))

    for y in range(4):
        pre = jnp.zeros((64, 128), F32)
        for i in range(3):
            pre = pre + dot(w3[i], rows_at(t3, i, y + 1))
        coarse_o[y] = silu(pre).astype(BF)
        cgrad_o[y] = (cot[y].astype(F32) * slope(pre)).astype(BF)


def middle_kernel(cgrad, t3, fpre, spre, craw_o, fslope_o, sslope_o):
    own = lane_mask(128, 0, 4, 68)
    raw = [jnp.zeros((64, 288), F32) for _ in range(3)]
    for y in range(4):
        mine = jnp.where(own > 0.5, cgrad[y].astype(F32), 0.0).astype(BF)
        for i in range(3):
            raw[i] = raw[i] + dot_lanes(mine, rows_at(t3, i, y + 1))
    for i in range(3):
        craw_o[i * 64 : (i + 1) * 64] = raw[i]

    def first(n, carry):
        for y in range(10):
            fslope_o[n, y] = slope(fpre[n, y])
        return carry

    def second(n, carry):
        for y in range(12):
            sslope_o[n, y] = slope(spre[n, y])
        return carry

    lax.fori_loop(0, 4, first, 0)
    lax.fori_loop(0, 6, second, 0)


def second_kernel(
    sizes, offs, cgrad, sslope, cot, t2, w3, spread, t5, sraw_o, t4, acc4, own5
):
    nx, ny, nz = sizes
    ox, oy, oz = offs[0], offs[1], offs[2]
    fine_ok = lane_mask(LANES, oz - 8, 0, nz)
    own_ok = lane_mask(LANES, 0, 8, 136)

    for x in range(5):
        for y in range(8):
            store_taps(t4, (x, y), cgrad[x, y].astype(F32))
    spread_conv(acc4, w3, t4, (0, 5), (1, 7), 32, 2)
    for x in (0, 1, 4, 5):
        own5[x] = jnp.zeros(own5.shape[1:], BF)
    matrix = spread[...]

    def second(n, carry):
        for cy in range(6):
            value = acc4[n + 2, cy + 1]
            high = value.astype(BF)
            low = (value - high.astype(F32)).astype(BF)
            wide = dot(high, matrix) + dot(low, matrix)
            for dx in range(2):
                for dy in range(2):
                    x, y = 2 * n + dx, 2 * cy + dy
                    grad = (cot[x, y].astype(F32) + wide) * sslope[x, y]
                    grad = keep(grad, fine_ok, (ox + x - 2, nx), (oy + y - 2, ny))
                    store_taps(t5, (x, y), grad.astype(BF).astype(F32))
        return carry

    lax.fori_loop(0, 3, second, 0)
    for x in range(2):
        for y in range(8):
            mine = t5[x + 2, y + 2, 32:64].astype(F32)
            own5[x + 2, y] = jnp.where(own_ok > 0.5, mine, 0.0).astype(BF)
    weight_sums(sraw_o, own5, t2)


def weight_sums(out, own, tapped):
    out[...] = jnp.zeros(out.shape, F32)

    def one(n, carry):
        total = jnp.zeros(out.shape, F32)
        for y in range(8):
            left = jnp.concatenate([own[n + 2, y], own[n + 1, y], own[n, y]], axis=0)
            total = total + dot_lanes(left, rows_at(tapped, n, y + 1))
        out[...] += total
        return carry

    lax.fori_loop(0, 4, one, 0)


def first_kernel(sizes, offs, t5, fslope, t1, w2, t6, thin_o, acc5, own6, fraw):
    nx, ny, nz = sizes
    ox, oy, oz = offs[0], offs[1], offs[2]
    fine_ok = lane_mask(LANES, oz - 8, 0, nz)
    own_ok = lane_mask(LANES, 0, 8, 136)
    for x in (0, 1, 4, 5):
        own6[x] = jnp.zeros(own6.shape[1:], BF)
    spread_conv(acc5, w2, t5, (0, 6), (1, 11), 32, 2)

    def first(n, carry):
        for y in range(10):
            grad = acc5[n + 2, y + 1] * fslope[n, y]
            grad = keep(grad, fine_ok, (ox + n - 1, nx), (oy + y - 1, ny))
            store_taps(t6, (n, y), grad.astype(BF).astype(F32))
        return carry

    lax.fori_loop(0, 4, first, 0)
    for x in range(2):
        for y in range(8):
            mine = t6[x + 1, y + 1, 32:64].astype(F32)
            own6[x + 2, y] = jnp.where(own_ok > 0.5, mine, 0.0).astype(BF)
    weight_sums(fraw, own6, t1)
    place = lax.broadcasted_iota(jnp.int32, (48, 128), 0)
    lane = lax.broadcasted_iota(jnp.int32, (48, 128), 1)
    term = place & 15
    column = jnp.where(term < 12, (place >> 4) * 12 + term, -200)
    thin = jnp.zeros((32, 128), F32)
    for i in range(3):
        picked = jnp.where(lane == column + 36 * i, 1.0, 0.0).astype(BF)
        thin = thin + dot(fraw[32 * i : 32 * i + 32].astype(BF), picked)
    thin_o[...] = thin.astype(BF)


def volume_kernel(t6, w1, vgrad_o):
    for x in range(2):
        for y in range(8):
            total = jnp.zeros((16, LANES), F32)
            for i in range(3):
                total = total + dot(w1[i], rows_at(t6, x + i, y + 1))
            vgrad_o[x, y] = pltpu.roll(total, LANES - 8, 1)[:, :128].astype(BF)


def flipped(weight):
    return jnp.transpose(weight[:, ::-1, ::-1, ::-1, :], (4, 1, 2, 3, 0))


def stacked(weight):
    outputs, chans = weight.shape[0], weight.shape[4]
    return jnp.transpose(weight, (1, 0, 2, 3, 4)).reshape(3, outputs, 9 * chans)


def swap(blocks, axes):
    return lax.all_to_all(blocks, axes, split_axis=0, concat_axis=0, tiled=True)


def added(blocks):
    return lax.optimization_barrier(jnp.sum(blocks.astype(F32), axis=0)).astype(BF)


def spread_rows(coarse_raw, second_raw):
    wide = jnp.concatenate([coarse_raw, second_raw], axis=0).astype(BF)
    piece = wide.shape[0] // 4
    rest = [wide[n * piece : (n + 1) * piece, 256:288] for n in range(4)]
    return jnp.concatenate(
        [wide[:, :128], wide[:, 128:256], jnp.concatenate(rest, axis=1)], axis=0
    )


def gathered_rows(rows):
    height, piece = 288, 72
    rest = rows[2 * height : 2 * height + piece]
    rest = jnp.concatenate([rest[:, 32 * n : 32 * n + 32] for n in range(4)], axis=0)
    wide = jnp.concatenate([rows[:height], rows[height : 2 * height], rest], axis=1)
    return wide[192:], wide[:192]


def plane_blocks(blocks):
    count = lax.axis_size("gy")
    place = lax.broadcasted_iota(jnp.int32, (count, 1, 1, 1), 0)
    mine = jnp.where(place == lax.axis_index("gy"), blocks[None], jnp.zeros((), blocks.dtype))
    return mine.reshape((count * blocks.shape[0],) + blocks.shape[1:])


def total_over_line(part):
    count = lax.axis_size("gx")
    for base in (1, 4):
        others = [
            lax.ppermute(part, "gx", [(i, i ^ step) for i in range(count)]).astype(F32)
            for step in (base, 2 * base, 3 * base)
            if step < count
        ]
        if len(others) == 3:
            total = (part.astype(F32) + others[0]) + (others[1] + others[2])
        elif others:
            total = part.astype(F32) + others[0]
        else:
            continue
        part = lax.optimization_barrier(total).astype(BF)
    return part


def weight_form(matrix, outputs, chans):
    return jnp.transpose(matrix.reshape(3, outputs, 3, 3, chans), (1, 0, 2, 3, 4))


def shape(dims, dtype):
    return jax.ShapeDtypeStruct(dims, dtype)


def local(volume, w_first, w_second, w_coarse, skip_cotangent, coarse_cotangent):
    counts = [lax.axis_size(axis) for axis in AXES]
    extents = volume.shape[1:]
    sizes = tuple(count * extent for count, extent in zip(counts, extents))
    offs = jnp.stack([lax.axis_index(axis) * extent for axis, extent in zip(AXES, extents)])
    offs = offs.astype(jnp.int32)

    rows_volume = jnp.transpose(volume, (1, 2, 0, 3))
    rows_cotangent = jnp.transpose(skip_cotangent, (1, 2, 0, 3))
    both = jnp.concatenate([rows_cotangent, rows_volume], axis=2)
    chans = skip_cotangent.shape[0]
    near = (shifted(both, "gx", 1), shifted(both, "gx", -1))
    far = (shifted(rows_volume, "gx", 2), shifted(rows_volume, "gx", -2))
    wide_volume = jnp.concatenate(
        [far[0], near[0][:, :, chans:], rows_volume, near[1][:, :, chans:], far[1]], axis=0
    )
    wide_volume = halo(halo(wide_volume, "gy", 1, 4), "gz", 3, 8)
    wide_volume = jnp.pad(wide_volume, ((0, 0), (0, 0), (0, 0), (0, LANES - 144)))
    tall_cotangent = jnp.concatenate(
        [near[0][:, :, :chans], rows_cotangent, near[1][:, :, :chans]], axis=0
    )
    tall_cotangent = halo(tall_cotangent, "gy", 1, 2)
    turned = (
        shifted(jnp.transpose(tall_cotangent[..., -2:], (0, 1, 3, 2)), "gz", 1),
        shifted(jnp.transpose(tall_cotangent[..., :2], (0, 1, 3, 2)), "gz", -1),
    )
    edges = [jnp.transpose(edge, (0, 1, 3, 2)) for edge in turned]
    wide_cotangent = jnp.concatenate([edges[0], tall_cotangent, edges[1]], axis=3)
    wide_cotangent = jnp.pad(wide_cotangent, ((0, 0), (0, 0), (0, 0), (6, LANES - 138)))
    sides = counts[2]
    depth = coarse_cotangent.shape[3] // sides
    guarded = jnp.pad(coarse_cotangent[:, 0], ((0, 0), (0, 0), (2, 2)))
    sent = jnp.stack([guarded[..., n * depth : n * depth + depth + 4] for n in range(sides)])
    returned = swap(sent, "gz")
    returned = jnp.transpose(returned, (2, 0, 1, 3)).reshape(4, 64, depth + 4)
    returned = jnp.pad(returned, ((0, 0), (0, 0), (2, 128 - 70)))
    returned = returned + wide_volume[0, 0, 0, 0] * 0
    fine_place = lax.broadcasted_iota(jnp.int32, (LANES, 128), 0)
    coarse_place = lax.broadcasted_iota(jnp.int32, (LANES, 128), 1)
    pool = jnp.where(fine_place // 2 == coarse_place, 1.0, 0.0).astype(BF)
    spread = jnp.transpose(pool) * 0.125

    thin_first = jnp.transpose(w_first, (1, 0, 2, 3, 4)).reshape(96, 3, 12)
    thin_first = jnp.pad(thin_first, ((0, 0), (0, 0), (0, 4))).reshape(96, 48)
    smem = pl.BlockSpec(memory_space=pltpu.SMEM)
    vmem = pl.BlockSpec(memory_space=pltpu.VMEM)
    skip, coarse_local, coarse_grad, taps3, first_pre, second_pre, taps1, taps2 = (
        pl.pallas_call(
            lambda *refs: forward_kernel(sizes, *refs),
            out_shape=(
                shape((2, 8, 32, 128), BF),
                shape((4, 64, 128), BF),
                shape((4, 64, 128), BF),
                shape((3, 6, 96, 128), BF),
                shape((4, 10, 32, LANES), F32),
                shape((6, 12, 32, LANES), F32),
                shape((4, 10, 16, LANES), BF),
                shape((4, 10, 96, LANES), BF),
            ),
            in_specs=[smem] + [vmem] * 6 + [pl.BlockSpec(memory_space=pl.ANY)] * 2,
            out_specs=(vmem,) * 8,
            scratch_shapes=[
                pltpu.VMEM((10, 16, 16, LANES), BF),
                pltpu.VMEM((12, 16, 32, LANES), F32),
                pltpu.VMEM((10, 16, 96, LANES), BF),
                pltpu.VMEM((12, 16, 32, LANES), F32),
                pltpu.VMEM((6, 12, 32, LANES), BF),
            ],
            compiler_params=pltpu.CompilerParams(vmem_limit_bytes=52 * 2**20),
            cost_estimate=pl.CostEstimate(
                flops=4 * 10**9, bytes_accessed=12 * 10**6, transcendentals=10**6
            ),
            name="forward",
        )(
            offs,
            wide_volume,
            thin_first,
            stacked(w_second).reshape(96, 288),
            stacked(w_coarse),
            returned,
            pool,
            *turned,
        )
    )
    coarse_raw, first_slope, second_slope = pl.pallas_call(
        middle_kernel,
        out_shape=(
            shape((192, 288), F32),
            shape((4, 10, 32, LANES), F32),
            shape((6, 12, 32, LANES), F32),
        ),
        in_specs=[vmem] * 4,
        out_specs=(vmem,) * 3,
        compiler_params=pltpu.CompilerParams(vmem_limit_bytes=48 * 2**20),
        cost_estimate=pl.CostEstimate(
            flops=10**9, bytes_accessed=10 * 10**6, transcendentals=10**6
        ),
        name="middle",
    )(coarse_grad, taps3, first_pre, second_pre)
    wide_grad = halo(halo(coarse_grad[None], "gx", 0, 2), "gy", 1, 2)
    taps5, second_raw = pl.pallas_call(
        lambda *refs: second_kernel(sizes, *refs),
        out_shape=(shape((6, 12, 96, LANES), BF), shape((96, 288), F32)),
        in_specs=[smem] + [vmem] * 6,
        out_specs=(vmem,) * 2,
        scratch_shapes=[
            pltpu.VMEM((5, 8, 192, 128), BF),
            pltpu.VMEM((7, 8, 32, 128), F32),
            pltpu.VMEM((6, 8, 32, LANES), BF),
        ],
        compiler_params=pltpu.CompilerParams(vmem_limit_bytes=48 * 2**20),
        cost_estimate=pl.CostEstimate(
            flops=10**9, bytes_accessed=10 * 10**6, transcendentals=10**6
        ),
        name="second",
    )(
        offs,
        wide_grad,
        second_slope,
        wide_cotangent,
        taps2,
        stacked(flipped(w_coarse)).reshape(96, 576),
        spread,
    )

    plane = ("gy", "gz")
    count = counts[1] * counts[2]
    rows = spread_rows(coarse_raw, second_raw)
    share = -(-rows.shape[0] // (8 * count)) * 8
    rows = jnp.pad(rows, ((0, share * count - rows.shape[0]), (0, 0)))
    blocks = coarse_local[:, :, 4 : 4 + depth].reshape(4, sides, 64 // sides, depth)
    blocks = jnp.transpose(blocks, (1, 0, 2, 3)).reshape(sides, -1, depth)
    half = blocks.shape[1] // 2
    blocks = jnp.concatenate([blocks[:, :half], blocks[:, half:]], axis=2)
    arrived = swap(
        jnp.concatenate([rows.reshape(count, share, 128), plane_blocks(blocks)], axis=1), plane
    )

    taps6, thin = pl.pallas_call(
        lambda *refs: first_kernel(sizes, *refs),
        out_shape=(shape((4, 10, 96, LANES), BF), shape((32, 128), BF)),
        in_specs=[smem] + [vmem] * 4,
        out_specs=(vmem,) * 2,
        scratch_shapes=[
            pltpu.VMEM((8, 12, 32, LANES), F32),
            pltpu.VMEM((6, 8, 32, LANES), BF),
            pltpu.VMEM((96, 48), F32),
        ],
        compiler_params=pltpu.CompilerParams(vmem_limit_bytes=48 * 2**20),
        cost_estimate=pl.CostEstimate(
            flops=2 * 10**9, bytes_accessed=10 * 10**6, transcendentals=10**6
        ),
        name="first",
    )(offs, taps5, first_slope, taps1, stacked(flipped(w_second)).reshape(96, 288))
    back_first = jnp.pad(flipped(w_first), ((0, 12),) + ((0, 0),) * 4)
    volume_grad = pl.pallas_call(
        volume_kernel,
        out_shape=shape((2, 8, 16, 128), BF),
        in_specs=[vmem] * 2,
        out_specs=vmem,
        compiler_params=pltpu.CompilerParams(vmem_limit_bytes=48 * 2**20),
        cost_estimate=pl.CostEstimate(
            flops=10**9, bytes_accessed=4 * 10**6, transcendentals=0
        ),
        name="volume",
    )(taps6, stacked(back_first))

    part = added(arrived[:, :share])
    own_row = lax.axis_index("gy") * sides
    coarse = lax.dynamic_slice_in_dim(arrived[:, share:], own_row, sides, axis=0)
    coarse = jnp.concatenate([coarse[:, :, :depth], coarse[:, :, depth:]], axis=1)
    coarse = coarse.reshape(sides, 4, 64 // sides, depth)
    coarse = jnp.transpose(coarse, (2, 1, 0, 3)).reshape(64 // sides, 1, 4, sides * depth)

    part = jnp.concatenate([part, thin], axis=0)
    part = total_over_line(part)
    whole = swap(jnp.broadcast_to(part, (count,) + part.shape), plane)
    second, wide = gathered_rows(whole[:, :share].reshape(count * share, 128).astype(F32))
    thin = jnp.sum(whole[:, share:].astype(F32), axis=0)
    thin = jnp.stack([thin[:, 36 * n : 36 * n + 36] for n in range(3)])

    skip = jnp.transpose(skip, (2, 0, 1, 3))
    volume_grad = jnp.transpose(volume_grad[:, :, :4], (2, 0, 1, 3))
    factor = 1.0 / math.sqrt(sizes[0] * sizes[1] * sizes[2])
    return (
        skip,
        coarse,
        volume_grad,
        weight_form(thin * factor, 32, 4),
        weight_form(second * factor, 32, 32),
        weight_form(wide * factor, 64, 32),
    )


def solution(mesh):
    in_specs = (
        P(None, "gx", "gy", "gz"),
        P(),
        P(),
        P(),
        P(None, "gx", "gy", "gz"),
        P("gz", "gx", "gy", None),
    )
    out_specs = (
        P(None, "gx", "gy", "gz"),
        P("gz", "gx", "gy", None),
        P(None, "gx", "gy", "gz"),
        P(),
        P(),
        P(),
    )
    return jax.shard_map(local, mesh=mesh, in_specs=in_specs, out_specs=out_specs, check_vma=False)
```

```python
import math

import jax
import jax.numpy as jnp
from jax import lax
from jax.experimental import pallas as pl
from jax.experimental.pallas import tpu as pltpu
from jax.sharding import PartitionSpec as P

AXES = ("gx", "gy", "gz")
LANES = 256
BF = jnp.bfloat16
F32 = jnp.float32


def shifted(block, axis, step):
    count = lax.axis_size(axis)
    pairs = [(i, i + step) for i in range(count) if 0 <= i + step < count]
    return lax.ppermute(block, axis, pairs)


def halo(cells, axis, dim, width):
    extent = cells.shape[dim]
    before, after = [], []
    for step in range(1, -(-width // extent) + 1):
        part = min(extent, width - (step - 1) * extent)
        tail = lax.slice_in_dim(cells, extent - part, extent, axis=dim)
        head = lax.slice_in_dim(cells, 0, part, axis=dim)
        before.insert(0, shifted(tail, axis, step))
        after.append(shifted(head, axis, -step))
    return jnp.concatenate(before + [cells] + after, axis=dim)


def slope(values):
    sigmoid_value = jax.nn.sigmoid(values)
    return sigmoid_value * (1.0 + values * (1.0 - sigmoid_value))


def silu(values):
    return values * jax.nn.sigmoid(values)


def store_taps(ref, place, values):
    chans, lanes = values.shape
    ref[place + (slice(0, chans),)] = pltpu.roll(values, 1, 1).astype(BF)
    ref[place + (slice(chans, 2 * chans),)] = values.astype(BF)
    ref[place + (slice(2 * chans, 3 * chans),)] = pltpu.roll(values, lanes - 1, 1).astype(BF)


def rows_at(ref, plane, row):
    part = ref[plane, row - 1 : row + 2]
    return part.reshape(part.shape[0] * part.shape[1], part.shape[2])


def dot(left, right):
    return jnp.dot(left, right, preferred_element_type=F32)


def dot_lanes(left, right):
    return lax.dot_general(left, right, (((1,), (1,)), ((), ())), preferred_element_type=F32)


def lane_mask(lanes, first, low, high):
    place = first + lax.broadcasted_iota(jnp.int32, (1, lanes), 1)
    return jnp.where((place >= low) & (place < high), 1.0, 0.0).astype(F32)


def keep(values, lanes_ok, *bounds):
    good = None
    for place, limit in bounds:
        here = (place >= 0) & (place < limit)
        good = here if good is None else good & here
    mask = lanes_ok * jnp.where(good, 1.0, 0.0).astype(F32)
    return jnp.where(mask > 0.5, values, 0.0)


def spread_conv(acc, weights, tapped, planes, rows, outputs, shift):
    matrix = weights[...]

    def one(n, carry):
        plane = planes[0] + n
        for row in range(*rows):
            summed = dot(matrix, rows_at(tapped, plane, row))
            acc[plane + shift, row] = summed[:outputs]
            for i in (1, 2):
                place = plane + shift - i
                acc[place, row] = acc[place, row] + summed[i * outputs : (i + 1) * outputs]
        return carry

    lax.fori_loop(0, planes[1] - planes[0], one, 0)


def forward_kernel(
    sizes, offs, vol, w1, w2, w3, cot, pool, unread_a, unread_b,
    skip_o, coarse_o, cgrad_o, t3, fpre_o, spre_o, t1_o, t2_o,
    t1, acc1, t2, acc2, fine,
):
    nx, ny, nz = sizes
    ox, oy, oz = offs[0], offs[1], offs[2]
    fine_ok = lane_mask(LANES, oz - 8, 0, nz)
    coarse_ok = lane_mask(128, oz // 2 - 4, 0, nz // 2)

    def volume_taps(x, carry):
        for y in range(16):
            here = vol[x, y].astype(F32)
            moved = [pltpu.roll(here, 1, 1), here, pltpu.roll(here, LANES - 1, 1)]
            t1[x, y] = jnp.concatenate(moved + [jnp.zeros_like(here)], axis=0).astype(BF)
        return carry

    lax.fori_loop(0, 10, volume_taps, 0)
    spread_conv(acc1, w1, t1, (0, 10), (1, 15), 32, 2)

    def first(n, carry):
        x = n + 1
        for y in range(1, 15):
            act = silu(acc1[x + 1, y])
            act = keep(act, fine_ok, (ox + x - 4, nx), (oy + y - 4, ny))
            store_taps(t2, (x, y), act.astype(BF).astype(F32))
        return carry

    lax.fori_loop(0, 8, first, 0)
    spread_conv(acc2, w2, t2, (1, 9), (2, 14), 32, 2)

    def second(n, carry):
        for y in range(12):
            pre = acc2[n + 3, y + 2]
            spre_o[n, y] = pre
            fine[n, y] = silu(pre).astype(BF)
        return carry

    lax.fori_loop(0, 6, second, 0)

    def passed(n, carry):
        for y in range(10):
            fpre_o[n, y] = acc1[n + 4, y + 3]
            t1_o[n, y] = t1[n + 3, y + 3]
            t2_o[n, y] = t2[n + 3, y + 3]
        return carry

    lax.fori_loop(0, 4, passed, 0)
    for x in range(2):
        for y in range(8):
            whole = pltpu.roll(fine[x + 2, y + 2].astype(F32), LANES - 8, 1)
            skip_o[x, y] = whole[:, :128].astype(BF)

    matrix = pool[...]
    for x in range(3):
        for y in range(6):
            cube = fine[2 * x : 2 * x + 2, 2 * y : 2 * y + 2].reshape(128, LANES)
            parts = dot(cube, matrix)
            mean = (parts[0:32] + parts[32:64] + parts[64:96] + parts[96:128]) * 0.125
            mean = keep(mean, coarse_ok, (ox // 2 + x - 1, nx // 2), (oy // 2 + y - 1, ny // 2))
            store_taps(t3, (x, y), mean.astype(BF).astype(F32))

    for y in range(4):
        pre = jnp.zeros((64, 128), F32)
        for i in range(3):
            pre = pre + dot(w3[i], rows_at(t3, i, y + 1))
        coarse_o[y] = silu(pre).astype(BF)
        cgrad_o[y] = (cot[y].astype(F32) * slope(pre)).astype(BF)


def middle_kernel(cgrad, t3, craw_o):
    own = lane_mask(128, 0, 4, 68)
    raw = [jnp.zeros((64, 288), F32) for _ in range(3)]
    for y in range(4):
        mine = jnp.where(own > 0.5, cgrad[y].astype(F32), 0.0).astype(BF)
        for i in range(3):
            raw[i] = raw[i] + dot_lanes(mine, rows_at(t3, i, y + 1))
    for i in range(3):
        craw_o[i * 64 : (i + 1) * 64] = raw[i]


def second_kernel(
    sizes, offs, cgrad, spre, cot, t2, w3, spread, t5, sraw_o, t4, acc4, own5
):
    nx, ny, nz = sizes
    ox, oy, oz = offs[0], offs[1], offs[2]
    fine_ok = lane_mask(LANES, oz - 8, 0, nz)
    own_ok = lane_mask(LANES, 0, 8, 136)

    for x in range(5):
        for y in range(8):
            store_taps(t4, (x, y), cgrad[x, y].astype(F32))
    spread_conv(acc4, w3, t4, (0, 5), (1, 7), 32, 2)
    for x in (0, 1, 4, 5):
        own5[x] = jnp.zeros(own5.shape[1:], BF)
    matrix = spread[...]

    def second(n, carry):
        for cy in range(6):
            value = acc4[n + 2, cy + 1]
            high = value.astype(BF)
            low = (value - high.astype(F32)).astype(BF)
            wide = dot(high, matrix) + dot(low, matrix)
            for dx in range(2):
                for dy in range(2):
                    x, y = 2 * n + dx, 2 * cy + dy
                    grad = (cot[x, y].astype(F32) + wide) * slope(spre[x, y])
                    grad = keep(grad, fine_ok, (ox + x - 2, nx), (oy + y - 2, ny))
                    store_taps(t5, (x, y), grad.astype(BF).astype(F32))
        return carry

    lax.fori_loop(0, 3, second, 0)
    for x in range(2):
        for y in range(8):
            mine = t5[x + 2, y + 2, 32:64].astype(F32)
            own5[x + 2, y] = jnp.where(own_ok > 0.5, mine, 0.0).astype(BF)
    weight_sums(sraw_o, own5, t2)


def weight_sums(out, own, tapped):
    out[...] = jnp.zeros(out.shape, F32)

    def one(n, carry):
        total = jnp.zeros(out.shape, F32)
        for y in range(8):
            left = jnp.concatenate([own[n + 2, y], own[n + 1, y], own[n, y]], axis=0)
            total = total + dot_lanes(left, rows_at(tapped, n, y + 1))
        out[...] += total
        return carry

    lax.fori_loop(0, 4, one, 0)


def first_kernel(sizes, offs, t5, fpre, t1, w2, t6, thin_o, acc5, own6, fraw):
    nx, ny, nz = sizes
    ox, oy, oz = offs[0], offs[1], offs[2]
    fine_ok = lane_mask(LANES, oz - 8, 0, nz)
    own_ok = lane_mask(LANES, 0, 8, 136)
    for x in (0, 1, 4, 5):
        own6[x] = jnp.zeros(own6.shape[1:], BF)
    spread_conv(acc5, w2, t5, (0, 6), (1, 11), 32, 2)

    def first(n, carry):
        for y in range(10):
            grad = acc5[n + 2, y + 1] * slope(fpre[n, y])
            grad = keep(grad, fine_ok, (ox + n - 1, nx), (oy + y - 1, ny))
            store_taps(t6, (n, y), grad.astype(BF).astype(F32))
        return carry

    lax.fori_loop(0, 4, first, 0)
    for x in range(2):
        for y in range(8):
            mine = t6[x + 1, y + 1, 32:64].astype(F32)
            own6[x + 2, y] = jnp.where(own_ok > 0.5, mine, 0.0).astype(BF)
    weight_sums(fraw, own6, t1)
    place = lax.broadcasted_iota(jnp.int32, (48, 128), 0)
    lane = lax.broadcasted_iota(jnp.int32, (48, 128), 1)
    term = place & 15
    column = jnp.where(term < 12, (place >> 4) * 12 + term, -200)
    thin = jnp.zeros((32, 128), F32)
    for i in range(3):
        picked = jnp.where(lane == column + 36 * i, 1.0, 0.0).astype(BF)
        thin = thin + dot(fraw[32 * i : 32 * i + 32].astype(BF), picked)
    thin_o[...] = thin.astype(BF)


def volume_kernel(t6, w1, vgrad_o):
    for x in range(2):
        for y in range(8):
            total = jnp.zeros((16, LANES), F32)
            for i in range(3):
                total = total + dot(w1[i], rows_at(t6, x + i, y + 1))
            vgrad_o[x, y] = pltpu.roll(total, LANES - 8, 1)[:, :128].astype(BF)


def flipped(weight):
    return jnp.transpose(weight[:, ::-1, ::-1, ::-1, :], (4, 1, 2, 3, 0))


def stacked(weight):
    outputs, chans = weight.shape[0], weight.shape[4]
    return jnp.transpose(weight, (1, 0, 2, 3, 4)).reshape(3, outputs, 9 * chans)


def swap(blocks, axes):
    return lax.all_to_all(blocks, axes, split_axis=0, concat_axis=0, tiled=True)


def added(blocks):
    return lax.optimization_barrier(jnp.sum(blocks.astype(F32), axis=0)).astype(BF)


def spread_rows(coarse_raw, second_raw):
    wide = jnp.concatenate([coarse_raw, second_raw], axis=0).astype(BF)
    piece = wide.shape[0] // 4
    rest = [wide[n * piece : (n + 1) * piece, 256:288] for n in range(4)]
    return jnp.concatenate(
        [wide[:, :128], wide[:, 128:256], jnp.concatenate(rest, axis=1)], axis=0
    )


def gathered_rows(rows):
    height, piece = 288, 72
    rest = rows[2 * height : 2 * height + piece]
    rest = jnp.concatenate([rest[:, 32 * n : 32 * n + 32] for n in range(4)], axis=0)
    wide = jnp.concatenate([rows[:height], rows[height : 2 * height], rest], axis=1)
    return wide[192:], wide[:192]


def plane_blocks(blocks):
    count = lax.axis_size("gy")
    place = lax.broadcasted_iota(jnp.int32, (count, 1, 1, 1), 0)
    mine = jnp.where(place == lax.axis_index("gy"), blocks[None], jnp.zeros((), blocks.dtype))
    return mine.reshape((count * blocks.shape[0],) + blocks.shape[1:])


def weight_form(matrix, outputs, chans):
    return jnp.transpose(matrix.reshape(3, outputs, 3, 3, chans), (1, 0, 2, 3, 4))


def shape(dims, dtype):
    return jax.ShapeDtypeStruct(dims, dtype)


def local(volume, w_first, w_second, w_coarse, skip_cotangent, coarse_cotangent):
    counts = [lax.axis_size(axis) for axis in AXES]
    extents = volume.shape[1:]
    sizes = tuple(count * extent for count, extent in zip(counts, extents))
    offs = jnp.stack([lax.axis_index(axis) * extent for axis, extent in zip(AXES, extents)])
    offs = offs.astype(jnp.int32)

    rows_volume = jnp.transpose(volume, (1, 2, 0, 3))
    rows_cotangent = jnp.transpose(skip_cotangent, (1, 2, 0, 3))
    both = jnp.concatenate([rows_cotangent, rows_volume], axis=2)
    chans = skip_cotangent.shape[0]
    near = (shifted(both, "gx", 1), shifted(both, "gx", -1))
    far = (shifted(rows_volume, "gx", 2), shifted(rows_volume, "gx", -2))
    wide_volume = jnp.concatenate(
        [far[0], near[0][:, :, chans:], rows_volume, near[1][:, :, chans:], far[1]], axis=0
    )
    wide_volume = halo(wide_volume, "gy", 1, 4)
    later = wide_volume[0, 0, 0, 0] * 0
    wide_volume = halo(wide_volume, "gz", 3, 8)
    wide_volume = jnp.pad(wide_volume, ((0, 0), (0, 0), (0, 0), (0, LANES - 144)))
    tall_cotangent = jnp.concatenate(
        [near[0][:, :, :chans], rows_cotangent, near[1][:, :, :chans]], axis=0
    )
    tall_cotangent = halo(tall_cotangent, "gy", 1, 2)
    turned = (
        shifted(jnp.transpose(tall_cotangent[..., -2:], (0, 1, 3, 2)), "gz", 1),
        shifted(jnp.transpose(tall_cotangent[..., :2], (0, 1, 3, 2)), "gz", -1),
    )
    edges = [jnp.transpose(edge, (0, 1, 3, 2)) for edge in turned]
    wide_cotangent = jnp.concatenate([edges[0], tall_cotangent, edges[1]], axis=3)
    wide_cotangent = jnp.pad(wide_cotangent, ((0, 0), (0, 0), (0, 0), (6, LANES - 138)))
    sides = counts[2]
    depth = coarse_cotangent.shape[3] // sides
    guarded = jnp.pad(coarse_cotangent[:, 0], ((0, 0), (0, 0), (2, 2)))
    sent = jnp.stack([guarded[..., n * depth : n * depth + depth + 4] for n in range(sides)])
    returned = swap(sent, "gz")
    returned = jnp.transpose(returned, (2, 0, 1, 3)).reshape(4, 64, depth + 4)
    returned = jnp.pad(returned, ((0, 0), (0, 0), (2, 128 - 70)))
    returned = returned + later
    fine_place = lax.broadcasted_iota(jnp.int32, (LANES, 128), 0)
    coarse_place = lax.broadcasted_iota(jnp.int32, (LANES, 128), 1)
    pool = jnp.where(fine_place // 2 == coarse_place, 1.0, 0.0).astype(BF)
    spread = jnp.transpose(pool) * 0.125

    thin_first = jnp.transpose(w_first, (1, 0, 2, 3, 4)).reshape(96, 3, 12)
    thin_first = jnp.pad(thin_first, ((0, 0), (0, 0), (0, 4))).reshape(96, 48)
    smem = pl.BlockSpec(memory_space=pltpu.SMEM)
    vmem = pl.BlockSpec(memory_space=pltpu.VMEM)
    skip, coarse_local, coarse_grad, taps3, first_pre, second_pre, taps1, taps2 = (
        pl.pallas_call(
            lambda *refs: forward_kernel(sizes, *refs),
            out_shape=(
                shape((2, 8, 32, 128), BF),
                shape((4, 64, 128), BF),
                shape((4, 64, 128), BF),
                shape((3, 6, 96, 128), BF),
                shape((4, 10, 32, LANES), F32),
                shape((6, 12, 32, LANES), F32),
                shape((4, 10, 16, LANES), BF),
                shape((4, 10, 96, LANES), BF),
            ),
            in_specs=[smem] + [vmem] * 6 + [pl.BlockSpec(memory_space=pl.ANY)] * 2,
            out_specs=(vmem,) * 8,
            scratch_shapes=[
                pltpu.VMEM((10, 16, 16, LANES), BF),
                pltpu.VMEM((12, 16, 32, LANES), F32),
                pltpu.VMEM((10, 16, 96, LANES), BF),
                pltpu.VMEM((12, 16, 32, LANES), F32),
                pltpu.VMEM((6, 12, 32, LANES), BF),
            ],
            compiler_params=pltpu.CompilerParams(vmem_limit_bytes=52 * 2**20),
            cost_estimate=pl.CostEstimate(
                flops=4 * 10**9, bytes_accessed=12 * 10**6, transcendentals=10**6
            ),
            name="forward",
        )(
            offs,
            wide_volume,
            thin_first,
            stacked(w_second).reshape(96, 288),
            stacked(w_coarse),
            returned,
            pool,
            *turned,
        )
    )
    coarse_raw = pl.pallas_call(
        middle_kernel,
        out_shape=shape((192, 288), F32),
        in_specs=[vmem] * 2,
        out_specs=vmem,
        compiler_params=pltpu.CompilerParams(vmem_limit_bytes=48 * 2**20),
        cost_estimate=pl.CostEstimate(
            flops=2 * 10**8, bytes_accessed=10**6, transcendentals=0
        ),
        name="middle",
    )(coarse_grad, taps3)
    wide_grad = halo(halo(coarse_grad[None], "gx", 0, 2), "gy", 1, 2)
    taps5, second_raw = pl.pallas_call(
        lambda *refs: second_kernel(sizes, *refs),
        out_shape=(shape((6, 12, 96, LANES), BF), shape((96, 288), F32)),
        in_specs=[smem] + [vmem] * 6,
        out_specs=(vmem,) * 2,
        scratch_shapes=[
            pltpu.VMEM((5, 8, 192, 128), BF),
            pltpu.VMEM((7, 8, 32, 128), F32),
            pltpu.VMEM((6, 8, 32, LANES), BF),
        ],
        compiler_params=pltpu.CompilerParams(vmem_limit_bytes=48 * 2**20),
        cost_estimate=pl.CostEstimate(
            flops=10**9, bytes_accessed=10 * 10**6, transcendentals=10**6
        ),
        name="second",
    )(
        offs,
        wide_grad,
        second_pre,
        wide_cotangent,
        taps2,
        stacked(flipped(w_coarse)).reshape(96, 576),
        spread,
    )

    plane = ("gy", "gz")
    count = counts[1] * counts[2]
    rows = spread_rows(coarse_raw, second_raw)
    share = -(-rows.shape[0] // (8 * count)) * 8
    rows = jnp.pad(rows, ((0, share * count - rows.shape[0]), (0, 0)))
    blocks = coarse_local[:, :, 4 : 4 + depth].reshape(4, sides, 64 // sides, depth)
    blocks = jnp.transpose(blocks, (1, 0, 2, 3)).reshape(sides, -1, depth)
    half = blocks.shape[1] // 2
    blocks = jnp.concatenate([blocks[:, :half], blocks[:, half:]], axis=2)
    arrived = swap(
        jnp.concatenate([rows.reshape(count, share, 128), plane_blocks(blocks)], axis=1), plane
    )

    taps6, thin = pl.pallas_call(
        lambda *refs: first_kernel(sizes, *refs),
        out_shape=(shape((4, 10, 96, LANES), BF), shape((32, 128), BF)),
        in_specs=[smem] + [vmem] * 4,
        out_specs=(vmem,) * 2,
        scratch_shapes=[
            pltpu.VMEM((8, 12, 32, LANES), F32),
            pltpu.VMEM((6, 8, 32, LANES), BF),
            pltpu.VMEM((96, 48), F32),
        ],
        compiler_params=pltpu.CompilerParams(vmem_limit_bytes=48 * 2**20),
        cost_estimate=pl.CostEstimate(
            flops=2 * 10**9, bytes_accessed=10 * 10**6, transcendentals=10**6
        ),
        name="first",
    )(offs, taps5, first_pre, taps1, stacked(flipped(w_second)).reshape(96, 288))
    back_first = jnp.pad(flipped(w_first), ((0, 12),) + ((0, 0),) * 4)
    volume_grad = pl.pallas_call(
        volume_kernel,
        out_shape=shape((2, 8, 16, 128), BF),
        in_specs=[vmem] * 2,
        out_specs=vmem,
        compiler_params=pltpu.CompilerParams(vmem_limit_bytes=48 * 2**20),
        cost_estimate=pl.CostEstimate(
            flops=10**9, bytes_accessed=4 * 10**6, transcendentals=0
        ),
        name="volume",
    )(taps6, stacked(back_first))

    part = added(arrived[:, :share])
    own_row = lax.axis_index("gy") * sides
    coarse = lax.dynamic_slice_in_dim(arrived[:, share:], own_row, sides, axis=0)
    coarse = jnp.concatenate([coarse[:, :, :depth], coarse[:, :, depth:]], axis=1)
    coarse = coarse.reshape(sides, 4, 64 // sides, depth)
    coarse = jnp.transpose(coarse, (2, 1, 0, 3)).reshape(64 // sides, 1, 4, sides * depth)

    part = jnp.concatenate([part, thin], axis=0)
    part = added(swap(jnp.broadcast_to(part, (counts[0],) + part.shape), "gx"))
    whole = swap(jnp.broadcast_to(part, (count,) + part.shape), plane)
    second, wide = gathered_rows(whole[:, :share].reshape(count * share, 128).astype(F32))
    thin = jnp.sum(whole[:, share:].astype(F32), axis=0)
    thin = jnp.stack([thin[:, 36 * n : 36 * n + 36] for n in range(3)])

    skip = jnp.transpose(skip, (2, 0, 1, 3))
    volume_grad = jnp.transpose(volume_grad[:, :, :4], (2, 0, 1, 3))
    factor = 1.0 / math.sqrt(sizes[0] * sizes[1] * sizes[2])
    return (
        skip,
        coarse,
        volume_grad,
        weight_form(thin * factor, 32, 4),
        weight_form(second * factor, 32, 32),
        weight_form(wide * factor, 64, 32),
    )


def solution(mesh):
    in_specs = (
        P(None, "gx", "gy", "gz"),
        P(),
        P(),
        P(),
        P(None, "gx", "gy", "gz"),
        P("gz", "gx", "gy", None),
    )
    out_specs = (
        P(None, "gx", "gy", "gz"),
        P("gz", "gx", "gy", None),
        P(None, "gx", "gy", "gz"),
        P(),
        P(),
        P(),
    )
    return jax.shard_map(local, mesh=mesh, in_specs=in_specs, out_specs=out_specs, check_vma=False)
```

```python
import math

import jax
import jax.numpy as jnp
from jax import lax
from jax.experimental import pallas as pl
from jax.experimental.pallas import tpu as pltpu
from jax.sharding import PartitionSpec as P

AXES = ("gx", "gy", "gz")
LANES = 256
BF = jnp.bfloat16
F32 = jnp.float32


def shifted(block, axis, step):
    count = lax.axis_size(axis)
    pairs = [(i, i + step) for i in range(count) if 0 <= i + step < count]
    return lax.ppermute(block, axis, pairs)


def halo(cells, axis, dim, width):
    extent = cells.shape[dim]
    before, after = [], []
    for step in range(1, -(-width // extent) + 1):
        part = min(extent, width - (step - 1) * extent)
        tail = lax.slice_in_dim(cells, extent - part, extent, axis=dim)
        head = lax.slice_in_dim(cells, 0, part, axis=dim)
        before.insert(0, shifted(tail, axis, step))
        after.append(shifted(head, axis, -step))
    return jnp.concatenate(before + [cells] + after, axis=dim)


def slope(values):
    sigmoid_value = jax.nn.sigmoid(values)
    return sigmoid_value * (1.0 + values * (1.0 - sigmoid_value))


def silu(values):
    return values * jax.nn.sigmoid(values)


def store_taps(ref, place, values):
    chans, lanes = values.shape
    ref[place + (slice(0, chans),)] = pltpu.roll(values, 1, 1).astype(BF)
    ref[place + (slice(chans, 2 * chans),)] = values.astype(BF)
    ref[place + (slice(2 * chans, 3 * chans),)] = pltpu.roll(values, lanes - 1, 1).astype(BF)


def rows_at(ref, plane, row):
    part = ref[plane, row - 1 : row + 2]
    return part.reshape(part.shape[0] * part.shape[1], part.shape[2])


def dot(left, right):
    return jnp.dot(left, right, preferred_element_type=F32)


def dot_lanes(left, right):
    return lax.dot_general(left, right, (((1,), (1,)), ((), ())), preferred_element_type=F32)


def lane_mask(lanes, first, low, high):
    place = first + lax.broadcasted_iota(jnp.int32, (1, lanes), 1)
    return jnp.where((place >= low) & (place < high), 1.0, 0.0).astype(F32)


def keep(values, lanes_ok, *bounds):
    good = None
    for place, limit in bounds:
        here = (place >= 0) & (place < limit)
        good = here if good is None else good & here
    mask = lanes_ok * jnp.where(good, 1.0, 0.0).astype(F32)
    return jnp.where(mask > 0.5, values, 0.0)


def spread_conv(acc, weights, tapped, planes, rows, outputs, shift):
    matrix = weights[...]

    def one(n, carry):
        plane = planes[0] + n
        for row in range(*rows):
            summed = dot(matrix, rows_at(tapped, plane, row))
            acc[plane + shift, row] = summed[:outputs]
            for i in (1, 2):
                place = plane + shift - i
                acc[place, row] = acc[place, row] + summed[i * outputs : (i + 1) * outputs]
        return carry

    lax.fori_loop(0, planes[1] - planes[0], one, 0)


def forward_kernel(
    sizes, offs, vol, w1, w2, w3, cot, pool, unread_a, unread_b,
    skip_o, coarse_o, cgrad_o, craw_o, fpre_o, spre_o, t1_o, t2_o,
    t1, acc1, t2, acc2, fine, t3,
):
    nx, ny, nz = sizes
    ox, oy, oz = offs[0], offs[1], offs[2]
    fine_ok = lane_mask(LANES, oz - 8, 0, nz)
    coarse_ok = lane_mask(128, oz // 2 - 4, 0, nz // 2)

    def volume_taps(x, carry):
        for y in range(16):
            here = vol[x, y].astype(F32)
            moved = [pltpu.roll(here, 1, 1), here, pltpu.roll(here, LANES - 1, 1)]
            t1[x, y] = jnp.concatenate(moved + [jnp.zeros_like(here)], axis=0).astype(BF)
        return carry

    lax.fori_loop(0, 10, volume_taps, 0)
    spread_conv(acc1, w1, t1, (0, 10), (1, 15), 32, 2)

    def first(n, carry):
        x = n + 1
        for y in range(1, 15):
            act = silu(acc1[x + 1, y])
            act = keep(act, fine_ok, (ox + x - 4, nx), (oy + y - 4, ny))
            store_taps(t2, (x, y), act.astype(BF).astype(F32))
        return carry

    lax.fori_loop(0, 8, first, 0)
    spread_conv(acc2, w2, t2, (1, 9), (2, 14), 32, 2)

    def second(n, carry):
        for y in range(12):
            pre = acc2[n + 3, y + 2]
            spre_o[n, y] = pre
            fine[n, y] = silu(pre).astype(BF)
        return carry

    lax.fori_loop(0, 6, second, 0)

    def passed(n, carry):
        for y in range(10):
            fpre_o[n, y] = acc1[n + 4, y + 3]
            t1_o[n, y] = t1[n + 3, y + 3]
            t2_o[n, y] = t2[n + 3, y + 3]
        return carry

    lax.fori_loop(0, 4, passed, 0)
    for x in range(2):
        for y in range(8):
            whole = pltpu.roll(fine[x + 2, y + 2].astype(F32), LANES - 8, 1)
            skip_o[x, y] = whole[:, :128].astype(BF)

    matrix = pool[...]
    for x in range(3):
        for y in range(6):
            cube = fine[2 * x : 2 * x + 2, 2 * y : 2 * y + 2].reshape(128, LANES)
            parts = dot(cube, matrix)
            mean = (parts[0:32] + parts[32:64] + parts[64:96] + parts[96:128]) * 0.125
            mean = keep(mean, coarse_ok, (ox // 2 + x - 1, nx // 2), (oy // 2 + y - 1, ny // 2))
            store_taps(t3, (x, y), mean.astype(BF).astype(F32))

    own = lane_mask(128, 0, 4, 68)
    raw = [jnp.zeros((64, 288), F32) for _ in range(3)]
    for y in range(4):
        pre = jnp.zeros((64, 128), F32)
        for i in range(3):
            pre = pre + dot(w3[i], rows_at(t3, i, y + 1))
        coarse_o[y] = silu(pre).astype(BF)
        grad = cot[y].astype(F32) * slope(pre)
        cgrad_o[y] = grad.astype(BF)
        mine = jnp.where(own > 0.5, grad, 0.0).astype(BF)
        for i in range(3):
            raw[i] = raw[i] + dot_lanes(mine, rows_at(t3, i, y + 1))
    for i in range(3):
        craw_o[i * 64 : (i + 1) * 64] = raw[i]


def second_kernel(
    sizes, offs, cgrad, spre, cot, t2, w3, spread, t5, sraw_o, t4, acc4, own5
):
    nx, ny, nz = sizes
    ox, oy, oz = offs[0], offs[1], offs[2]
    fine_ok = lane_mask(LANES, oz - 8, 0, nz)
    own_ok = lane_mask(LANES, 0, 8, 136)

    for x in range(5):
        for y in range(8):
            store_taps(t4, (x, y), cgrad[x, y].astype(F32))
    spread_conv(acc4, w3, t4, (0, 5), (1, 7), 32, 2)
    for x in (0, 1, 4, 5):
        own5[x] = jnp.zeros(own5.shape[1:], BF)
    matrix = spread[...]

    def second(n, carry):
        for cy in range(6):
            value = acc4[n + 2, cy + 1]
            high = value.astype(BF)
            low = (value - high.astype(F32)).astype(BF)
            wide = dot(high, matrix) + dot(low, matrix)
            for dx in range(2):
                for dy in range(2):
                    x, y = 2 * n + dx, 2 * cy + dy
                    grad = (cot[x, y].astype(F32) + wide) * slope(spre[x, y])
                    grad = keep(grad, fine_ok, (ox + x - 2, nx), (oy + y - 2, ny))
                    store_taps(t5, (x, y), grad.astype(BF).astype(F32))
        return carry

    lax.fori_loop(0, 3, second, 0)
    for x in range(2):
        for y in range(8):
            mine = t5[x + 2, y + 2, 32:64].astype(F32)
            own5[x + 2, y] = jnp.where(own_ok > 0.5, mine, 0.0).astype(BF)
    weight_sums(sraw_o, own5, t2)


def weight_sums(out, own, tapped):
    out[...] = jnp.zeros(out.shape, F32)

    def one(n, carry):
        total = jnp.zeros(out.shape, F32)
        for y in range(8):
            left = jnp.concatenate([own[n + 2, y], own[n + 1, y], own[n, y]], axis=0)
            total = total + dot_lanes(left, rows_at(tapped, n, y + 1))
        out[...] += total
        return carry

    lax.fori_loop(0, 4, one, 0)


def first_kernel(sizes, offs, t5, fpre, t1, w2, t6, thin_o, acc5, own6, fraw):
    nx, ny, nz = sizes
    ox, oy, oz = offs[0], offs[1], offs[2]
    fine_ok = lane_mask(LANES, oz - 8, 0, nz)
    own_ok = lane_mask(LANES, 0, 8, 136)
    for x in (0, 1, 4, 5):
        own6[x] = jnp.zeros(own6.shape[1:], BF)
    spread_conv(acc5, w2, t5, (0, 6), (1, 11), 32, 2)

    def first(n, carry):
        for y in range(10):
            grad = acc5[n + 2, y + 1] * slope(fpre[n, y])
            grad = keep(grad, fine_ok, (ox + n - 1, nx), (oy + y - 1, ny))
            store_taps(t6, (n, y), grad.astype(BF).astype(F32))
        return carry

    lax.fori_loop(0, 4, first, 0)
    for x in range(2):
        for y in range(8):
            mine = t6[x + 1, y + 1, 32:64].astype(F32)
            own6[x + 2, y] = jnp.where(own_ok > 0.5, mine, 0.0).astype(BF)
    weight_sums(fraw, own6, t1)
    place = lax.broadcasted_iota(jnp.int32, (48, 128), 0)
    lane = lax.broadcasted_iota(jnp.int32, (48, 128), 1)
    term = place & 15
    column = jnp.where(term < 12, (place >> 4) * 12 + term, -200)
    thin = jnp.zeros((32, 128), F32)
    for i in range(3):
        picked = jnp.where(lane == column + 36 * i, 1.0, 0.0).astype(BF)
        thin = thin + dot(fraw[32 * i : 32 * i + 32].astype(BF), picked)
    thin_o[...] = thin.astype(BF)


def volume_kernel(t6, w1, vgrad_o):
    for x in range(2):
        for y in range(8):
            total = jnp.zeros((16, LANES), F32)
            for i in range(3):
                total = total + dot(w1[i], rows_at(t6, x + i, y + 1))
            vgrad_o[x, y] = pltpu.roll(total, LANES - 8, 1)[:, :128].astype(BF)


def flipped(weight):
    return jnp.transpose(weight[:, ::-1, ::-1, ::-1, :], (4, 1, 2, 3, 0))


def stacked(weight):
    outputs, chans = weight.shape[0], weight.shape[4]
    return jnp.transpose(weight, (1, 0, 2, 3, 4)).reshape(3, outputs, 9 * chans)


def swap(blocks, axes):
    return lax.all_to_all(blocks, axes, split_axis=0, concat_axis=0, tiled=True)


def added(blocks):
    return lax.optimization_barrier(jnp.sum(blocks.astype(F32), axis=0)).astype(BF)


def spread_rows(coarse_raw, second_raw):
    wide = jnp.concatenate([coarse_raw, second_raw], axis=0).astype(BF)
    piece = wide.shape[0] // 4
    rest = [wide[n * piece : (n + 1) * piece, 256:288] for n in range(4)]
    return jnp.concatenate(
        [wide[:, :128], wide[:, 128:256], jnp.concatenate(rest, axis=1)], axis=0
    )


def gathered_rows(rows):
    height, piece = 288, 72
    rest = rows[2 * height : 2 * height + piece]
    rest = jnp.concatenate([rest[:, 32 * n : 32 * n + 32] for n in range(4)], axis=0)
    wide = jnp.concatenate([rows[:height], rows[height : 2 * height], rest], axis=1)
    return wide[192:], wide[:192]


def plane_blocks(blocks):
    count = lax.axis_size("gy")
    place = lax.broadcasted_iota(jnp.int32, (count, 1, 1, 1), 0)
    mine = jnp.where(place == lax.axis_index("gy"), blocks[None], jnp.zeros((), blocks.dtype))
    return mine.reshape((count * blocks.shape[0],) + blocks.shape[1:])


def weight_form(matrix, outputs, chans):
    return jnp.transpose(matrix.reshape(3, outputs, 3, 3, chans), (1, 0, 2, 3, 4))


def shape(dims, dtype):
    return jax.ShapeDtypeStruct(dims, dtype)


def local(volume, w_first, w_second, w_coarse, skip_cotangent, coarse_cotangent):
    counts = [lax.axis_size(axis) for axis in AXES]
    extents = volume.shape[1:]
    sizes = tuple(count * extent for count, extent in zip(counts, extents))
    offs = jnp.stack([lax.axis_index(axis) * extent for axis, extent in zip(AXES, extents)])
    offs = offs.astype(jnp.int32)

    rows_volume = jnp.transpose(volume, (1, 2, 0, 3))
    rows_cotangent = jnp.transpose(skip_cotangent, (1, 2, 0, 3))
    both = jnp.concatenate([rows_cotangent, rows_volume], axis=2)
    chans = skip_cotangent.shape[0]
    near = (shifted(both, "gx", 1), shifted(both, "gx", -1))
    far = (shifted(rows_volume, "gx", 2), shifted(rows_volume, "gx", -2))
    wide_volume = jnp.concatenate(
        [far[0], near[0][:, :, chans:], rows_volume, near[1][:, :, chans:], far[1]], axis=0
    )
    wide_volume = halo(wide_volume, "gy", 1, 4)
    later = wide_volume[0, 0, 0, 0] * 0
    wide_volume = halo(wide_volume, "gz", 3, 8)
    wide_volume = jnp.pad(wide_volume, ((0, 0), (0, 0), (0, 0), (0, LANES - 144)))
    tall_cotangent = jnp.concatenate(
        [near[0][:, :, :chans], rows_cotangent, near[1][:, :, :chans]], axis=0
    )
    tall_cotangent = halo(tall_cotangent, "gy", 1, 2)
    turned = (
        shifted(jnp.transpose(tall_cotangent[..., -2:], (0, 1, 3, 2)), "gz", 1),
        shifted(jnp.transpose(tall_cotangent[..., :2], (0, 1, 3, 2)), "gz", -1),
    )
    edges = [jnp.transpose(edge, (0, 1, 3, 2)) for edge in turned]
    wide_cotangent = jnp.concatenate([edges[0], tall_cotangent, edges[1]], axis=3)
    wide_cotangent = jnp.pad(wide_cotangent, ((0, 0), (0, 0), (0, 0), (6, LANES - 138)))
    sides = counts[2]
    depth = coarse_cotangent.shape[3] // sides
    guarded = jnp.pad(coarse_cotangent[:, 0], ((0, 0), (0, 0), (2, 2)))
    sent = jnp.stack([guarded[..., n * depth : n * depth + depth + 4] for n in range(sides)])
    returned = swap(sent, "gz") + later
    returned = jnp.transpose(returned, (2, 0, 1, 3)).reshape(4, 64, depth + 4)
    returned = jnp.pad(returned, ((0, 0), (0, 0), (2, 128 - 70)))
    fine_place = lax.broadcasted_iota(jnp.int32, (LANES, 128), 0)
    coarse_place = lax.broadcasted_iota(jnp.int32, (LANES, 128), 1)
    pool = jnp.where(fine_place // 2 == coarse_place, 1.0, 0.0).astype(BF)
    spread = jnp.transpose(pool) * 0.125

    thin_first = jnp.transpose(w_first, (1, 0, 2, 3, 4)).reshape(96, 3, 12)
    thin_first = jnp.pad(thin_first, ((0, 0), (0, 0), (0, 4))).reshape(96, 48)
    smem = pl.BlockSpec(memory_space=pltpu.SMEM)
    vmem = pl.BlockSpec(memory_space=pltpu.VMEM)
    skip, coarse_local, coarse_grad, coarse_raw, first_pre, second_pre, taps1, taps2 = (
        pl.pallas_call(
            lambda *refs: forward_kernel(sizes, *refs),
            out_shape=(
                shape((2, 8, 32, 128), BF),
                shape((4, 64, 128), BF),
                shape((4, 64, 128), BF),
                shape((192, 288), F32),
                shape((4, 10, 32, LANES), F32),
                shape((6, 12, 32, LANES), F32),
                shape((4, 10, 16, LANES), BF),
                shape((4, 10, 96, LANES), BF),
            ),
            in_specs=[smem] + [vmem] * 6 + [pl.BlockSpec(memory_space=pl.ANY)] * 2,
            out_specs=(vmem,) * 8,
            scratch_shapes=[
                pltpu.VMEM((10, 16, 16, LANES), BF),
                pltpu.VMEM((12, 16, 32, LANES), F32),
                pltpu.VMEM((10, 16, 96, LANES), BF),
                pltpu.VMEM((12, 16, 32, LANES), F32),
                pltpu.VMEM((6, 12, 32, LANES), BF),
                pltpu.VMEM((3, 6, 96, 128), BF),
            ],
            compiler_params=pltpu.CompilerParams(vmem_limit_bytes=52 * 2**20),
            cost_estimate=pl.CostEstimate(
                flops=4 * 10**9, bytes_accessed=12 * 10**6, transcendentals=10**6
            ),
            name="forward",
        )(
            offs,
            wide_volume,
            thin_first,
            stacked(w_second).reshape(96, 288),
            stacked(w_coarse),
            returned,
            pool,
            *turned,
        )
    )
    wide_grad = halo(halo(coarse_grad[None], "gx", 0, 2), "gy", 1, 2)
    taps5, second_raw = pl.pallas_call(
        lambda *refs: second_kernel(sizes, *refs),
        out_shape=(shape((6, 12, 96, LANES), BF), shape((96, 288), F32)),
        in_specs=[smem] + [vmem] * 6,
        out_specs=(vmem,) * 2,
        scratch_shapes=[
            pltpu.VMEM((5, 8, 192, 128), BF),
            pltpu.VMEM((7, 8, 32, 128), F32),
            pltpu.VMEM((6, 8, 32, LANES), BF),
        ],
        compiler_params=pltpu.CompilerParams(vmem_limit_bytes=48 * 2**20),
        cost_estimate=pl.CostEstimate(
            flops=10**9, bytes_accessed=10 * 10**6, transcendentals=10**6
        ),
        name="second",
    )(
        offs,
        wide_grad,
        second_pre,
        wide_cotangent,
        taps2,
        stacked(flipped(w_coarse)).reshape(96, 576),
        spread,
    )

    plane = ("gy", "gz")
    count = counts[1] * counts[2]
    rows = spread_rows(coarse_raw, second_raw)
    share = -(-rows.shape[0] // (8 * count)) * 8
    rows = jnp.pad(rows, ((0, share * count - rows.shape[0]), (0, 0)))
    blocks = coarse_local[:, :, 4 : 4 + depth].reshape(4, sides, 64 // sides, depth)
    blocks = jnp.transpose(blocks, (1, 0, 2, 3)).reshape(sides, -1, depth)
    half = blocks.shape[1] // 2
    blocks = jnp.concatenate([blocks[:, :half], blocks[:, half:]], axis=2)
    arrived = swap(
        jnp.concatenate([rows.reshape(count, share, 128), plane_blocks(blocks)], axis=1), plane
    )

    taps6, thin = pl.pallas_call(
        lambda *refs: first_kernel(sizes, *refs),
        out_shape=(shape((4, 10, 96, LANES), BF), shape((32, 128), BF)),
        in_specs=[smem] + [vmem] * 4,
        out_specs=(vmem,) * 2,
        scratch_shapes=[
            pltpu.VMEM((8, 12, 32, LANES), F32),
            pltpu.VMEM((6, 8, 32, LANES), BF),
            pltpu.VMEM((96, 48), F32),
        ],
        compiler_params=pltpu.CompilerParams(vmem_limit_bytes=48 * 2**20),
        cost_estimate=pl.CostEstimate(
            flops=2 * 10**9, bytes_accessed=10 * 10**6, transcendentals=10**6
        ),
        name="first",
    )(offs, taps5, first_pre, taps1, stacked(flipped(w_second)).reshape(96, 288))
    back_first = jnp.pad(flipped(w_first), ((0, 12),) + ((0, 0),) * 4)
    volume_grad = pl.pallas_call(
        volume_kernel,
        out_shape=shape((2, 8, 16, 128), BF),
        in_specs=[vmem] * 2,
        out_specs=vmem,
        compiler_params=pltpu.CompilerParams(vmem_limit_bytes=48 * 2**20),
        cost_estimate=pl.CostEstimate(
            flops=10**9, bytes_accessed=4 * 10**6, transcendentals=0
        ),
        name="volume",
    )(taps6, stacked(back_first))

    part = added(arrived[:, :share])
    own_row = lax.axis_index("gy") * sides
    coarse = lax.dynamic_slice_in_dim(arrived[:, share:], own_row, sides, axis=0)
    coarse = jnp.concatenate([coarse[:, :, :depth], coarse[:, :, depth:]], axis=1)
    coarse = coarse.reshape(sides, 4, 64 // sides, depth)
    coarse = jnp.transpose(coarse, (2, 1, 0, 3)).reshape(64 // sides, 1, 4, sides * depth)

    part = jnp.concatenate([part, thin], axis=0)
    part = added(swap(jnp.broadcast_to(part, (counts[0],) + part.shape), "gx"))
    whole = swap(jnp.broadcast_to(part, (count,) + part.shape), plane)
    second, wide = gathered_rows(whole[:, :share].reshape(count * share, 128).astype(F32))
    thin = jnp.sum(whole[:, share:].astype(F32), axis=0)
    thin = jnp.stack([thin[:, 36 * n : 36 * n + 36] for n in range(3)])

    skip = jnp.transpose(skip, (2, 0, 1, 3))
    volume_grad = jnp.transpose(volume_grad[:, :, :4], (2, 0, 1, 3))
    factor = 1.0 / math.sqrt(sizes[0] * sizes[1] * sizes[2])
    return (
        skip,
        coarse,
        volume_grad,
        weight_form(thin * factor, 32, 4),
        weight_form(second * factor, 32, 32),
        weight_form(wide * factor, 64, 32),
    )


def solution(mesh):
    in_specs = (
        P(None, "gx", "gy", "gz"),
        P(),
        P(),
        P(),
        P(None, "gx", "gy", "gz"),
        P("gz", "gx", "gy", None),
    )
    out_specs = (
        P(None, "gx", "gy", "gz"),
        P("gz", "gx", "gy", None),
        P(None, "gx", "gy", "gz"),
        P(),
        P(),
        P(),
    )
    return jax.shard_map(local, mesh=mesh, in_specs=in_specs, out_specs=out_specs, check_vma=False)
```
